32 devices in a mesh: view: 4 (over y, x), tile: 8 (over z, core).
Axes of the slice: x: 2, y: 2, z: 4, core: 2. Of those that a mesh axis runs over, the one named last changes fastest.
Arguments:
- estimate: float32 [128, 192, 512], P(None, 'tile'), may hold values from 0.5 to 2
- view_stacks: float32 [4, 128, 192, 512], P('view', 'tile'), may hold values from 0 to 4
- profile_z: float32 [4, 31], P('view'), may hold values from 0.2 to 1
- profile_y: float32 [4, 15], P('view'), may hold values from 0.2 to 1
- profile_x: float32 [4, 15], P('view'), may hold values from 0.2 to 1
- offsets: int32 [4], P('view'), may hold values from -16 to 16, as said below
- coverage: int32 [8, 4], P('tile'), may hold values from 0 to 1, as said below
Outputs:
- new_estimate: float32 [128, 192, 512], P(None, 'tile')
The draws below stay inside these ranges and needn't reach their ends.
Inputs may be any that keep to these rules, and one draw needn't show every extreme that they name: `offsets`: some view has offset 16 and some view has offset -16. `coverage`: every tile is intersected by at least one view.
All inputs are finite; a program needn't handle non-finite values.
Results may differ from the reference program's by a relative error of at most 0.0001.
Values sent between devices are 32-bit elements; how exact they have to be, the bound alone decides.
No kernel may reach another device: no remote copies, remote signals or barrier semaphores. Data moves between devices by JAX's collectives and lax.ppermute only.
A program may use at most 192 MiB of HBM per device.

```python
import math
import jax
import jax.numpy as jnp
from jax import lax

Z = 128
YD = 24
X = 512
KZ = 31
KY = 15
KX = 15
MAXOFF = 16
VIEWS = 4
TILES = 8
Y = 192


def draw_offsets(key, part):
    base = jax.random.randint(key, (VIEWS,), -MAXOFF, MAXOFF + 1)
    order = jax.random.permutation(jax.random.fold_in(key, 7), VIEWS)
    base = base.at[order[0]].set(MAXOFF)
    base = base.at[order[1]].set(-MAXOFF)
    return base.astype(jnp.int32)


def draw_coverage(key, part):
    first = jax.random.fold_in(key, 11)
    second = jax.random.fold_in(key, 13)
    levels = jax.random.randint(first, (TILES, VIEWS), 0, 5)
    bits = (levels < 3).astype(jnp.int32)
    chosen = jax.random.randint(second, (TILES,), 0, VIEWS)
    columns = jnp.arange(VIEWS, dtype=jnp.int32)
    onehot = (columns[None, :] == chosen[:, None]).astype(jnp.int32)
    return jnp.maximum(bits, onehot).astype(jnp.int32)


def block_scale(stream_key, shape, shards, smallest, largest):
    level, own = 1.0, jax.random.fold_in(stream_key, 6)
    for axis_at, blocks in shards:
        draws = jnp.exp(jax.random.uniform(jax.random.fold_in(own, axis_at), (blocks,), jnp.float32, smallest / len(shards), largest / len(shards)))
        level = level * jnp.repeat(draws, shape[axis_at] // blocks).reshape([-1 if axis == axis_at else 1 for axis in range(len(shape))])
    return level


def setup_inputs(seed: int = 0) -> dict:
    seeds = jax.random.split(jax.random.key(seed), 8)
    estimate = jnp.clip(0.5 + 1.5 * jax.random.uniform(seeds[0], (Z, Y, X), jnp.float32) ** block_scale(seeds[0], (Z, Y, X), ((1, 8),), -0.2, 0.2), 0.5, 2.0)
    view_stacks = jnp.clip(4.0 * jax.random.uniform(seeds[1], (VIEWS, Z, Y, X), jnp.float32) ** block_scale(seeds[1], (VIEWS, Z, Y, X), ((0, 4), (1, 8)), -0.2, 0.2), 0.0, 4.0)
    profile_z = jnp.clip(jnp.exp(math.log(1.0) - 1.609438 * jax.random.uniform(seeds[2], (VIEWS, KZ), jnp.float32) ** block_scale(seeds[2], (VIEWS, KZ), ((0, 4),), -0.2, 0.2)), 0.2, 1.0)
    profile_y = jnp.clip(jnp.exp(math.log(1.0) - 1.609438 * jax.random.uniform(seeds[3], (VIEWS, KY), jnp.float32) ** block_scale(seeds[3], (VIEWS, KY), ((0, 4),), -0.2, 0.2)), 0.2, 1.0)
    profile_x = jnp.clip(jnp.exp(math.log(1.0) - 1.609438 * jax.random.uniform(seeds[4], (VIEWS, KX), jnp.float32) ** block_scale(seeds[4], (VIEWS, KX), ((0, 4),), -0.2, 0.2)), 0.2, 1.0)
    offsets = draw_offsets(jax.random.fold_in(seeds[7], 71), 0)
    coverage = draw_coverage(jax.random.fold_in(seeds[7], 71), 0)
    return {"estimate": estimate, "view_stacks": view_stacks, "profile_z": profile_z, "profile_y": profile_y, "profile_x": profile_x, "offsets": offsets, "coverage": coverage}


def correlate(field, kernel, along):
    taps_count = kernel.shape[0]
    half = (taps_count - 1) // 2
    widths = [(0, 0), (0, 0), (0, 0)]
    widths[along] = (half, half)
    padded = jnp.pad(field, widths)
    extent = field.shape[along]
    summed = jnp.zeros(field.shape, jnp.float32)
    for tap_index in range(taps_count):
        summed = summed + kernel[tap_index] * lax.slice_in_dim(padded, tap_index, tap_index + extent, axis=along)
    return summed


def blur_three(field, weights_z, weights_y, weights_x):
    result = correlate(field, weights_z, 0)
    result = correlate(result, weights_y, 1)
    return correlate(result, weights_x, 2)


def reference(estimate, view_stacks, profile_z, profile_y, profile_x, offsets, coverage):
    view_count = jnp.sum(coverage, axis=1).astype(jnp.float32)
    merged = jnp.zeros(estimate.shape, jnp.float32)
    for view_id in range(VIEWS):
        weights_z = profile_z[view_id] / jnp.sum(profile_z[view_id])
        weights_y = profile_y[view_id] / jnp.sum(profile_y[view_id])
        weights_x = profile_x[view_id] / jnp.sum(profile_x[view_id])
        padded = jnp.pad(view_stacks[view_id], ((0, 0), (0, 0), (MAXOFF, MAXOFF)))
        start = (MAXOFF + offsets[view_id]).astype(jnp.int32)
        registered = lax.dynamic_slice_in_dim(padded, start, X, 2)
        blurred = blur_three(estimate, weights_z, weights_y, weights_x)
        quotient = registered / blurred
        back_blur = blur_three(quotient, weights_z[::-1], weights_y[::-1], weights_x[::-1])
        tile_weight = jnp.repeat(coverage[:, view_id].astype(jnp.float32), YD)
        merged = merged + tile_weight[None, :, None] * back_blur
    tile_count = jnp.repeat(view_count, YD)
    return estimate * merged / tile_count[None, :, None]
```

```python
import functools

import jax
import jax.numpy as jnp
from jax import lax
from jax.experimental import pallas as pl
from jax.experimental.pallas import tpu as pltpu
from jax.sharding import PartitionSpec as P

LANES = 128
F32 = jnp.float32
BF16 = jnp.bfloat16
SMEM = pl.BlockSpec(memory_space=pltpu.SMEM)
VMEM = pl.BlockSpec(memory_space=pltpu.VMEM)
ANY = pl.BlockSpec(memory_space=pl.ANY)


def sds(shape, dtype=F32):
    return jax.ShapeDtypeStruct(shape, dtype)


def params(mib):
    return pltpu.CompilerParams(vmem_limit_bytes=mib << 20)


def split(value):
    high = value.astype(BF16)
    return high, (value - high.astype(F32)).astype(BF16)


def dot(a, b):
    return jnp.dot(a, b, preferred_element_type=F32)


def prep_kernel(lead, scalars, stack_ref, *out_refs):
    planes, rows, cells = stack_ref.shape
    offset = scalars[0]
    lane = lax.broadcasted_iota(jnp.int32, (1, 1, cells), 2)
    column = lane + lead
    column = jnp.where(column >= cells, column - cells, column)
    source = column + offset
    inside = (source >= 0) & (source < cells)
    shift = lax.rem(2 * cells - lead - offset, cells)
    rolled = pltpu.roll(stack_ref[...].reshape(planes * rows, cells), shift, 1)
    rolled = jnp.where(inside, rolled.reshape(planes, rows, cells), 0.0)
    for index, out_ref in enumerate(out_refs):
        out_ref[0] = rolled[:, :, index * LANES : (index + 1) * LANES]


def prep(stack, offset, tiles, lead):
    planes, all_rows, cells = stack.shape
    rows = all_rows // tiles
    count = cells // LANES
    return pl.pallas_call(
        functools.partial(prep_kernel, lead),
        grid=(tiles,),
        in_specs=[SMEM, pl.BlockSpec((planes, rows, cells), lambda i: (0, i, 0))],
        out_specs=[pl.BlockSpec((1, planes, rows, LANES), lambda i: (i, 0, 0, 0))] * count,
        out_shape=[sds((tiles, planes, rows, LANES))] * count,
        compiler_params=params(32),
        name="prep",
    )(offset, stack)


def swap_kernel(in_ref, out_ref):
    out_ref[...] = jnp.swapaxes(in_ref[...], 0, 1)


def swap(cells):
    planes, rows, width = cells.shape
    return pl.pallas_call(
        swap_kernel,
        grid=(planes // 16,),
        in_specs=[pl.BlockSpec((16, rows, width), lambda i: (i, 0, 0))],
        out_specs=pl.BlockSpec((rows, 16, width), lambda i: (0, i, 0)),
        out_shape=sds((rows, planes, width)),
        name="swap",
    )(cells)


def place_rows(even, own, inner, outer, buffer, sems, half):
    rows = own.shape[0]
    inner_at = jnp.where(even == 1, half + rows, 0)
    outer_at = jnp.where(even == 1, 0, half + rows)
    copies = [
        pltpu.make_async_copy(own, buffer.at[pl.ds(half, rows)], sems.at[0]),
        pltpu.make_async_copy(inner, buffer.at[pl.ds(inner_at, half)], sems.at[1]),
        pltpu.make_async_copy(outer, buffer.at[pl.ds(outer_at, half)], sems.at[2]),
    ]
    for copy in copies:
        copy.start()
    for copy in copies:
        copy.wait()


def blur_y(buffer, weights, taps, rows, planes_at, lanes_at):
    at = (pl.ds(planes_at, 16), pl.ds(lanes_at, LANES))
    cells = [buffer[(r, *at)] for r in range(rows + taps - 1)]
    for r in range(rows):
        total = weights[0] * cells[r]
        for tap in range(1, taps):
            total = total + weights[tap] * cells[r + tap]
        yield r, split(total)


def forward_kernel(taps, scalars, weights, own, inner, outer, along_z, high_x, low_x, out_ref, buffer, halves, sems):
    rows, planes, cells = own.shape
    half = (taps - 1) // 2
    place_rows(scalars[0], own, inner, outer, buffer, sems, half)

    def step_y(index, carry):
        planes_at = pl.multiple_of((index // (cells // LANES)) * 16, 16)
        lanes_at = pl.multiple_of((index % (cells // LANES)) * LANES, LANES)
        for r, (high, low) in blur_y(buffer, weights, taps, rows, planes_at, lanes_at):
            halves[r, pl.ds(planes_at, 16), pl.ds(lanes_at, LANES)] = high
            halves[r, pl.ds(planes + planes_at, 16), pl.ds(lanes_at, LANES)] = low
        return carry

    lax.fori_loop(0, (planes // 16) * (cells // LANES), step_y, 0)
    group = 4

    def step_zx(index, carry):
        parts = []
        for g in range(group):
            both = dot(along_z[...], halves[index * group + g])
            parts.append(both[:planes] + both[planes:])
        high, low = split(jnp.concatenate(parts, axis=0))
        result = dot(high, high_x[...]) + dot(low, high_x[...]) + dot(high, low_x[...])
        out_ref[pl.ds(index * group, group)] = result.reshape(group, planes, cells)
        return carry

    lax.fori_loop(0, rows // group, step_zx, 0)


def forward(even, weights, own, inner, outer, along_z, high_x, low_x):
    rows, planes, cells = own.shape
    taps = weights.shape[0]
    return pl.pallas_call(
        functools.partial(forward_kernel, taps),
        in_specs=[SMEM, SMEM, ANY, ANY, ANY, VMEM, VMEM, VMEM],
        out_specs=VMEM,
        out_shape=sds((rows, planes, cells)),
        scratch_shapes=[
            pltpu.VMEM((rows + taps - 1, planes, cells), F32),
            pltpu.VMEM((rows, 2 * planes, cells), BF16),
            pltpu.SemaphoreType.DMA((3,)),
        ],
        compiler_params=params(48),
        cost_estimate=pl.CostEstimate(flops=20_000_000_000, bytes_accessed=20_000_000, transcendentals=0),
        name="forward",
    )(even, weights, own, inner, outer, along_z, high_x, low_x)


def ratio_kernel(half, scalars, measured_ref, blurred_ref, out_ref, inner_ref, outer_ref):
    rows = out_ref.shape[0]
    ratio = jnp.swapaxes(measured_ref[...], 0, 1) / blurred_ref[...]
    out_ref[...] = ratio
    even = scalars[0]
    first, last = ratio[:half], ratio[rows - half :]
    inner_ref[...] = jnp.where(even == 1, last, first)
    outer_ref[...] = jnp.where(even == 1, first, last)


def ratio(even, measured, blurred, half, chunk):
    planes, rows, _ = measured.shape
    return pl.pallas_call(
        functools.partial(ratio_kernel, half),
        grid=(planes // 16,),
        in_specs=[
            SMEM,
            pl.BlockSpec((16, rows, LANES), lambda i: (i, 0, 0)),
            pl.BlockSpec((rows, 16, LANES), lambda i: (0, i, chunk)),
        ],
        out_specs=[
            pl.BlockSpec((rows, 16, LANES), lambda i: (0, i, 0)),
            pl.BlockSpec((half, 16, LANES), lambda i: (0, i, 0)),
            pl.BlockSpec((half, 16, LANES), lambda i: (0, i, 0)),
        ],
        out_shape=[
            sds((rows, planes, LANES)),
            sds((half, planes, LANES)),
            sds((half, planes, LANES)),
        ],
        cost_estimate=pl.CostEstimate(flops=1_000_000, bytes_accessed=6_000_000, transcendentals=0),
        name="ratio",
    )(even, measured, blurred)


def back_kernel(taps, blocks, scalars, weights, own, inner, outer, along_z, *refs):
    rows, planes, _ = own.shape
    half = (taps - 1) // 2
    ins = 3 * len(blocks)
    extra, refs = refs[:ins], refs[ins:]
    high_ref, low_ref, refs = refs[0], refs[1], refs[2:]
    quarters, refs = refs[: 4 * len(blocks)], refs[4 * len(blocks) :]
    buffer, halves, totals, sems, out_sems = refs
    place_rows(scalars[0], own, inner, outer, buffer, sems, half)

    def step_y(index, carry):
        planes_at = pl.multiple_of(index * 16, 16)
        for r, (high, low) in blur_y(buffer, weights, taps, rows, planes_at, 0):
            lanes = slice((r % 2) * LANES, (r % 2 + 1) * LANES)
            halves[r // 2, pl.ds(planes_at, 16), lanes] = high
            halves[r // 2, pl.ds(planes + planes_at, 16), lanes] = low
        return carry

    lax.fori_loop(0, planes // 16, step_y, 0)
    group = 4

    def step_zx(index, carry):
        parts = []
        for g in range(group // 2):
            both = dot(along_z[...], halves[index * (group // 2) + g])
            both = both[:planes] + both[planes:]
            parts += [both[:, :LANES], both[:, LANES:]]
        high, low = split(jnp.concatenate(parts, axis=0))
        at = pl.ds(index * group, group)
        high_ref[at] = high.reshape(group, planes, LANES)
        low_ref[at] = low.reshape(group, planes, LANES)
        for number, (_, after) in enumerate(blocks):
            other_high, other_low, along_x = extra[3 * number : 3 * number + 3]
            others = [other_high[at].reshape(-1, LANES), other_low[at].reshape(-1, LANES)]
            result = 0.0
            for mine, other in zip((high, low), others):
                pair = [mine, other] if after else [other, mine]
                result = result + dot(jnp.concatenate(pair, axis=1), along_x[...])
            result = result[:, :LANES] + result[:, LANES:]
            totals[number, at] = result.reshape(group, planes, LANES)
        return carry

    lax.fori_loop(0, rows // group, step_zx, 0)
    copies = []
    size = planes // 4
    for number in range(len(blocks)):
        for k in range(4):
            start = pl.multiple_of((scalars[1] ^ k) * size, size)
            copies.append(
                pltpu.make_async_copy(
                    totals.at[number, :, pl.ds(start, size)], quarters[4 * number + k], out_sems.at[number, k]
                )
            )
    for copy in copies:
        copy.start()
    for copy in copies:
        copy.wait()


def back(scalars, weights, own, inner, outer, along_z, blocks, extra):
    rows, planes, _ = own.shape
    taps = weights.shape[0]
    count = len(blocks)
    outs = pl.pallas_call(
        functools.partial(back_kernel, taps, blocks),
        in_specs=[SMEM, SMEM, ANY, ANY, ANY, VMEM] + [VMEM] * (3 * count),
        out_specs=[VMEM] * 2 + [ANY] * (4 * count),
        out_shape=[sds((rows, planes, LANES), BF16)] * 2
        + [sds((rows, planes // 4, LANES))] * (4 * count),
        scratch_shapes=[
            pltpu.VMEM((rows + taps - 1, planes, LANES), F32),
            pltpu.VMEM((rows // 2, 2 * planes, 2 * LANES), BF16),
            pltpu.VMEM((max(count, 1), rows, planes, LANES), F32),
            pltpu.SemaphoreType.DMA((3,)),
            pltpu.SemaphoreType.DMA((max(count, 1), 4)),
        ],
        compiler_params=params(32),
        cost_estimate=pl.CostEstimate(flops=5_000_000_000, bytes_accessed=6_000_000, transcendentals=0),
        name="back",
    )(scalars, weights, own, inner, outer, along_z, *extra)
    return outs[0], outs[1], [outs[2 + 4 * n : 6 + 4 * n] for n in range(count)]


def merge_kernel(scalars, estimate_ref, a, b, c, d, out_ref):
    total = (a[...] + b[...]) + (c[...] + d[...])
    count = scalars[2].astype(F32)
    out_ref[...] = estimate_ref[...] * jnp.swapaxes(total, 0, 1) / count


def merge(scalars, estimate, parts, chunk):
    rows, size, _ = parts[0].shape
    step = 16
    steps = size // step
    piece = pl.BlockSpec((rows, step, LANES), lambda i, s: (0, i, 0))
    return pl.pallas_call(
        merge_kernel,
        grid_spec=pltpu.PrefetchScalarGridSpec(
            num_scalar_prefetch=1,
            grid=(steps,),
            in_specs=[pl.BlockSpec((step, rows, LANES), lambda i, s: (s[1] * steps + i, 0, chunk))]
            + [piece] * 4,
            out_specs=pl.BlockSpec((step, rows, LANES), lambda i, s: (i, 0, 0)),
        ),
        out_shape=sds((size, rows, LANES)),
        cost_estimate=pl.CostEstimate(flops=1_000_000, bytes_accessed=3_000_000, transcendentals=0),
        name="merge",
    )(scalars, estimate, *parts)


def assemble_kernel(chunk, scalars, *refs):
    pieces, out_ref, sems = refs[:4], refs[-2], refs[-1]
    size = pieces[0].shape[0]
    copies = [
        pltpu.make_async_copy(
            piece,
            out_ref.at[pl.ds((scalars[1] ^ k) * size, size), :, pl.ds(chunk * LANES, LANES)],
            sems.at[k],
        )
        for k, piece in enumerate(pieces)
    ]
    for copy in copies:
        copy.start()
    for copy in copies:
        copy.wait()


def assemble(scalars, pieces, shape, chunk, result):
    earlier = [] if result is None else [result]
    return pl.pallas_call(
        functools.partial(assemble_kernel, chunk),
        in_specs=[SMEM] + [VMEM] * 4 + [ANY] * len(earlier),
        out_specs=ANY,
        out_shape=sds(shape),
        scratch_shapes=[pltpu.SemaphoreType.DMA((4,))],
        input_output_aliases={} if result is None else {5: 0},
        cost_estimate=pl.CostEstimate(flops=0, bytes_accessed=3_000_000, transcendentals=0),
        name="assemble",
    )(scalars, *pieces, *earlier)


def taps_at(distance, profile):
    result = jnp.zeros(distance.shape, F32)
    for tap in range(profile.shape[1]):
        result = jnp.where(distance == tap, profile[0, tap], result)
    return result


def total_of(profile):
    total = profile[0, 0]
    for tap in range(1, profile.shape[1]):
        total = total + profile[0, tap]
    return total


def bands_kernel(scalars, profile_z, profile_y, profile_x, forward_z, back_z, high_x, low_x, back_x):
    planes = forward_z.shape[0] // 2
    cells = high_x.shape[0]
    half_z = (profile_z.shape[1] - 1) // 2
    lead = (profile_x.shape[1] - 1) // 2
    total_z, total_y, total_x = total_of(profile_z), total_of(profile_y), total_of(profile_x)
    row = lax.broadcasted_iota(jnp.int32, (planes, planes), 0)
    column = lax.broadcasted_iota(jnp.int32, (planes, planes), 1)
    for out, distance in ((forward_z, column - row), (back_z, row - column)):
        high, low = split(taps_at(distance + half_z, profile_z) / total_z / total_y)
        for side in (slice(0, planes), slice(planes, 2 * planes)):
            out[:planes, side] = high
            out[planes:, side] = low

    step = 32

    def step_x(index, carry):
        at = pl.multiple_of(index * step, step)
        row = lax.broadcasted_iota(jnp.int32, (step, cells), 0) + at
        column = lax.broadcasted_iota(jnp.int32, (step, cells), 1) + lead
        column = jnp.where(column >= cells, column - cells, column)
        high, low = split(taps_at(row - column + lead, profile_x) / total_x)
        high_x[pl.ds(at, step), :] = high
        low_x[pl.ds(at, step), :] = low
        return carry

    lax.fori_loop(0, cells // step, step_x, 0)
    row = lax.broadcasted_iota(jnp.int32, (2 * LANES, LANES), 0)
    column = lax.broadcasted_iota(jnp.int32, (2 * LANES, LANES), 1)
    matrix = taps_at(column + LANES - row, profile_x) / total_x * scalars[3].astype(F32)
    for block in range(back_x.shape[0]):
        source = row + ((block - 1) * LANES + lead)
        high, low = split(jnp.where((source >= 0) & (source < cells), matrix, 0.0))
        back_x[block, :, :LANES] = high
        back_x[block, :, LANES:] = low


def bands(scalars, profile_z, profile_y, profile_x, planes, cells):
    return pl.pallas_call(
        bands_kernel,
        in_specs=[SMEM] * 4,
        out_specs=[VMEM] * 5,
        out_shape=[
            sds((2 * planes, 2 * planes), BF16),
            sds((2 * planes, 2 * planes), BF16),
            sds((cells, cells), BF16),
            sds((cells, cells), BF16),
            sds((cells // LANES, 2 * LANES, 2 * LANES), BF16),
        ],
        name="bands",
    )(scalars, profile_z, profile_y, profile_x)


def swap_views(cells, mask):
    return lax.ppermute(cells, "view", [(i, i ^ mask) for i in range(4)])


def on_device(estimate, view_stacks, profile_z, profile_y, profile_x, offsets, coverage):
    planes, rows, cells = estimate.shape
    half = (profile_y.shape[1] - 1) // 2
    lead = (profile_x.shape[1] - 1) // 2
    tiles = lax.axis_size("tile")
    tile = lax.axis_index("tile")
    view = lax.axis_index("view")
    chunks = cells // LANES
    even = (tile + 1) % 2
    covered = lax.dynamic_index_in_dim(coverage[0], view, 0, keepdims=False)
    scalars = jnp.stack([even, view, jnp.sum(coverage[0]), covered]).astype(jnp.int32)
    inner_pairs = [(i, i ^ 1) for i in range(tiles)]
    outer_pairs = [(i, i + 1) for i in range(1, tiles - 1, 2)] + [(i + 1, i) for i in range(1, tiles - 1, 2)]

    def exchange(inner, outer):
        return lax.ppermute(inner, "tile", inner_pairs), lax.ppermute(outer, "tile", outer_pairs)

    registered = prep(view_stacks[0], offsets, tiles, lead)

    forward_z, back_z, high_x, low_x, back_x = bands(scalars, profile_z, profile_y, profile_x, planes, cells)
    transposed = swap(estimate)
    first, last = transposed[:half], transposed[rows - half :]
    is_even = even == 1
    inner, outer = exchange(jnp.where(is_even, last, first), jnp.where(is_even, first, last))
    blurred = forward(scalars, profile_y[0], transposed, inner, outer, forward_z, high_x, low_x)

    flipped = profile_y[0, ::-1]
    order = [chunks - 1] + list(range(chunks - 1))
    done = {}
    result = None
    for chunk in order:
        measured = lax.all_to_all(registered[chunk], "tile", split_axis=0, concat_axis=0)
        measured = measured.reshape(planes, rows, LANES)
        quotient, inner, outer = ratio(scalars, measured, blurred, half, chunk)
        inner, outer = exchange(inner, outer)
        blocks, extra = [], []
        for block in (chunk, (chunk + 1) % chunks):
            other = (block - 1) % chunks if block == chunk else block
            if other in done:
                blocks.append((block, block != chunk))
                extra += [done[other][0], done[other][1], back_x[block]]
        high, low, sums = back(scalars, flipped, quotient, inner, outer, back_z, tuple(blocks), extra)
        done[chunk] = (high, low)
        for (block, _), parts in zip(blocks, sums):
            received = [parts[0]] + [swap_views(parts[k], k) for k in (1, 2, 3)]
            new = merge(scalars, estimate, received, block)
            pieces = [new] + [swap_views(new, k) for k in (1, 2, 3)]
            result = assemble(scalars, pieces, estimate.shape, block, result)
    return result


def solution(mesh):
    return jax.shard_map(
        on_device,
        mesh=mesh,
        in_specs=(
            P(None, "tile", None),
            P("view", "tile", None, None),
            P("view", None),
            P("view", None),
            P("view", None),
            P("view"),
            P("tile", None),
        ),
        out_specs=P(None, "tile", None),
        check_vma=False,
    )
```

```python
import functools

import jax
import jax.numpy as jnp
from jax import lax
from jax.experimental import pallas as pl
from jax.experimental.pallas import tpu as pltpu
from jax.sharding import PartitionSpec as P

LANES = 128
SLOT = 8
VMEM_MIB = 56
F32 = jnp.float32
BF16 = jnp.bfloat16
SMEM = pl.BlockSpec(memory_space=pltpu.SMEM)
VMEM = pl.BlockSpec(memory_space=pltpu.VMEM)
ANY = pl.BlockSpec(memory_space=pl.ANY)


MICROS = dict(prep=9, edge_rows=5, swap=8, swap_edges=6, gate=1, forward=30, ratio=5, back=60, bands=4, merge=30, assemble=10)


def cost(name):
    micros = MICROS[name]
    return pl.CostEstimate(flops=int(micros * 1.1e9), bytes_accessed=int(micros * 3.6e6), transcendentals=0)


def sds(shape, dtype=F32):
    return jax.ShapeDtypeStruct(shape, dtype)


def params():
    return pltpu.CompilerParams(vmem_limit_bytes=VMEM_MIB << 20)


def split(value):
    high = value.astype(BF16)
    return high, (value - high.astype(F32)).astype(BF16)


def dot(a, b):
    return jnp.dot(a, b, preferred_element_type=F32)


def pack(rows):
    lane = lax.broadcasted_iota(jnp.int32, rows[0].shape, 1)
    total = jnp.zeros(rows[0].shape, F32)
    for slot, row in enumerate(rows):
        moved = pltpu.roll(row, (SLOT * slot + SLOT) % LANES, 1)
        total = jnp.where((lane >= SLOT * slot) & (lane < SLOT * slot + SLOT), moved, total)
    return total


def unpack(packed, slot):
    lane = lax.broadcasted_iota(jnp.int32, packed.shape, 1)
    moved = pltpu.roll(packed, (2 * LANES - SLOT - SLOT * slot) % LANES, 1)
    return jnp.where(lane >= LANES - SLOT, moved, 0.0)


def prep_kernel(lead, groups, offsets, stack_ref, after, *out_refs):
    *out_refs, token_ref = out_refs
    token_ref[...] = jnp.zeros(token_ref.shape, F32)
    planes, rows, cells = stack_ref.shape
    offset = offsets[0]
    lane = lax.broadcasted_iota(jnp.int32, (1, 1, cells), 2)
    column = lane + lead
    column = jnp.where(column >= cells, column - cells, column)
    source = column + offset
    inside = (source >= 0) & (source < cells)
    shift = lax.rem(2 * cells - lead - offset, cells)
    rolled = pltpu.roll(stack_ref[...].reshape(planes * rows, cells), shift, 1)
    rolled = jnp.where(inside, rolled.reshape(planes, rows, cells), 0.0)
    size = planes * rows
    for group, out_ref in zip(groups, out_refs):
        for number, chunk in enumerate(group):
            values = rolled[:, :, chunk * LANES : (chunk + 1) * LANES]
            out_ref[0, number * size : (number + 1) * size] = values.reshape(size, LANES)
    tail = rolled[:, :, cells - LANES :]
    per = LANES // SLOT
    for number in range(pl.cdiv(rows, per)):
        at = len(groups[0]) * size + number * planes
        members = range(number * per, min((number + 1) * per, rows))
        out_refs[0][0, at : at + planes] = pack([tail[:, r, :] for r in members])


def prep(offsets, stack, tiles, lead, groups, after):
    planes, all_rows, cells = stack.shape
    rows = all_rows // tiles
    sizes = [len(group) * planes * rows for group in groups]
    sizes[0] += planes * pl.cdiv(rows, LANES // SLOT)
    return pl.pallas_call(
        functools.partial(prep_kernel, lead, groups),
        grid=(tiles,),
        in_specs=[SMEM, pl.BlockSpec((planes, rows, cells), lambda i: (0, i, 0)), ANY],
        out_specs=[pl.BlockSpec((1, size, LANES), lambda i: (i, 0, 0)) for size in sizes]
        + [pl.BlockSpec((8, LANES), lambda i: (0, 0))],
        out_shape=[sds((tiles, size, LANES)) for size in sizes] + [sds((8, LANES))],
        compiler_params=params(),
        cost_estimate=cost("prep"),
        name="prep",
    )(offsets, stack, after)


def copy_kernel(scalars, first_ref, second_ref, inner_ref, outer_ref):
    inner_ref[...] = first_ref[...]

    @pl.when(pl.program_id(0) == 0)
    def _():
        outer_ref[...] = second_ref[...]


def edge_rows(places, cells):
    planes, rows, width = cells.shape
    last = rows // 8 - 1
    step = planes // 4
    return pl.pallas_call(
        copy_kernel,
        grid_spec=pltpu.PrefetchScalarGridSpec(
            num_scalar_prefetch=1,
            grid=(planes // step,),
            in_specs=[
                pl.BlockSpec((step, 8, width), lambda i, s: (i, s[0] * last, 0)),
                pl.BlockSpec((step, 8, width), lambda i, s: (s[1], (1 - s[0]) * last, 0)),
            ],
            out_specs=[
                pl.BlockSpec((step, 8, width), lambda i, s: (i, 0, 0)),
                pl.BlockSpec((step, 8, width), lambda i, s: (0, 0, 0)),
            ],
        ),
        out_shape=[sds((planes, 8, width)), sds((step, 8, width))],
        compiler_params=params(),
        cost_estimate=cost("edge_rows"),
        name="edge_rows",
    )(places, cells, cells)


def swap_kernel(in_ref, after, out_ref):
    out_ref[...] = jnp.swapaxes(in_ref[...], 0, 1)


def swap(cells, after):
    planes, rows, width = cells.shape
    return pl.pallas_call(
        swap_kernel,
        grid=(planes // 16,),
        in_specs=[pl.BlockSpec((16, rows, width), lambda i: (i, 0, 0)), ANY],
        out_specs=pl.BlockSpec((rows, 16, width), lambda i: (0, i, 0)),
        out_shape=sds((rows, planes, width)),
        compiler_params=params(),
        cost_estimate=cost("swap"),
        name="swap",
    )(cells, after)


def swap_edges_kernel(half, scalars, inner_ref, a, b, c, d, after, inner_out, outer_out):
    even = scalars[0]
    inner = jnp.swapaxes(inner_ref[...], 0, 1)
    skip = inner.shape[0] - half
    inner_out[...] = jnp.where(even == 1, inner[:half], inner[skip:])
    for k, piece in enumerate((a, b, c, d)):

        @pl.when(pl.program_id(0) == k)
        def _():
            outer = jnp.swapaxes(piece[...], 0, 1)
            outer_out[...] = jnp.where(even == 1, outer[skip:], outer[:half])


def swap_edges(places, inner, pieces, half, after):
    planes, rows, width = inner.shape
    step = planes // 4
    return pl.pallas_call(
        functools.partial(swap_edges_kernel, half),
        grid_spec=pltpu.PrefetchScalarGridSpec(
            num_scalar_prefetch=1,
            grid=(4,),
            in_specs=[pl.BlockSpec((step, rows, width), lambda i, s: (s[1] ^ i, 0, 0))]
            + [pl.BlockSpec((step, rows, width), lambda i, s: (0, 0, 0))] * 4
            + [ANY],
            out_specs=[pl.BlockSpec((half, step, width), lambda i, s: (0, s[1] ^ i, 0))] * 2,
        ),
        out_shape=[sds((half, planes, width))] * 2,
        compiler_params=params(),
        cost_estimate=cost("swap_edges"),
        name="swap_edges",
    )(places, inner, *pieces, after)


def gate_kernel(*refs):
    pass


def gate(arrays, after):
    count = len(arrays)
    return pl.pallas_call(
        gate_kernel,
        in_specs=[ANY] * (count + len(after)),
        out_specs=[ANY] * count,
        out_shape=[sds(array.shape) for array in arrays],
        input_output_aliases={i: i for i in range(count)},
        compiler_params=params(),
        cost_estimate=cost("gate"),
        name="gate",
    )(*arrays, *after)


def place_rows(even, own, inner, outer, edges_at, buffer, sems, half):
    rows, planes, _ = own.shape
    blocks = sems.shape[1]
    step = planes // blocks
    inner_at = jnp.where(even == 1, half + rows, 0)
    outer_at = jnp.where(even == 1, 0, half + rows)
    copies = []
    for block in range(blocks):
        at = pl.ds(block * step, step)
        edge = pl.ds(edges_at, half)
        copies.append(
            [
                pltpu.make_async_copy(own.at[:, at], buffer.at[pl.ds(half, rows), at], sems.at[0, block]),
                pltpu.make_async_copy(inner.at[edge, at], buffer.at[pl.ds(inner_at, half), at], sems.at[1, block]),
                pltpu.make_async_copy(outer.at[edge, at], buffer.at[pl.ds(outer_at, half), at], sems.at[2, block]),
            ]
        )
    return copies


def start_all(copies):
    for copy in copies:
        copy.start()


def wait_all(copies):
    for copy in copies:
        copy.wait()


def blur_y(buffer, weights, taps, rows, planes_at, lanes_at):
    at = (pl.ds(planes_at, 16), pl.ds(lanes_at, LANES))
    cells = [buffer[(r, *at)] for r in range(rows + taps - 1)]
    for r in range(rows):
        total = weights[0] * cells[r]
        for tap in range(1, taps):
            total = total + weights[tap] * cells[r + tap]
        yield r, split(total)


def forward_kernel(taps, scalars, weights, own, inner, outer, along_z, high_x, low_x, after, out_ref, buffer, halves, sems):
    rows, planes, cells = own.shape
    half = (taps - 1) // 2
    blocks = place_rows(scalars[0], own, inner, outer, 0, buffer, sems, half)
    for copies in blocks:
        start_all(copies)
    step = planes // len(blocks)
    for block, copies in enumerate(blocks):
        wait_all(copies)

        def step_y(index, carry):
            planes_at = pl.multiple_of(block * step + (index // (cells // LANES)) * 16, 16)
            lanes_at = pl.multiple_of((index % (cells // LANES)) * LANES, LANES)
            for r, (high, low) in blur_y(buffer, weights, taps, rows, planes_at, lanes_at):
                halves[r, pl.ds(planes_at, 16), pl.ds(lanes_at, LANES)] = high
                halves[r, pl.ds(planes + planes_at, 16), pl.ds(lanes_at, LANES)] = low
            return carry

        lax.fori_loop(0, (step // 16) * (cells // LANES), step_y, 0)
    group = 4

    def step_zx(index, carry):
        parts = []
        for g in range(group):
            both = dot(along_z[...], halves[index * group + g])
            parts.append(both[:planes] + both[planes:])
        high, low = split(jnp.concatenate(parts, axis=0))
        result = dot(high, high_x[...]) + dot(low, high_x[...]) + dot(high, low_x[...])
        out_ref[pl.ds(index * group, group)] = result.reshape(group, planes, cells)
        return carry

    lax.fori_loop(0, rows // group, step_zx, 0)


def forward(even, weights, own, inner, outer, along_z, high_x, low_x, after):
    rows, planes, cells = own.shape
    taps = weights.shape[0]
    return pl.pallas_call(
        functools.partial(forward_kernel, taps),
        in_specs=[SMEM, SMEM, ANY, ANY, ANY, VMEM, VMEM, VMEM, ANY],
        out_specs=VMEM,
        out_shape=sds((rows, planes, cells)),
        scratch_shapes=[
            pltpu.VMEM((rows + taps - 1, planes, cells), F32),
            pltpu.VMEM((rows, 2 * planes, cells), BF16),
            pltpu.SemaphoreType.DMA((3, 4)),
        ],
        compiler_params=params(),
        cost_estimate=cost("forward"),
        name="forward",
    )(even, weights, own, inner, outer, along_z, high_x, low_x, after)


def edges_of(cells, half):
    return cells[:half], cells[cells.shape[0] - half :]


def ratio_kernel(half, chunks, first, scalars, moved_ref, *refs):
    count = len(chunks)
    blurred_refs, refs = refs[:count], refs[count:]
    if first:
        tail_ref, _, *refs = refs
        tail_out, packed = refs[count + 2 :]
    else:
        _, *refs = refs
    out_refs = refs[:count]
    inner_ref, outer_ref = refs[count : count + 2]
    rows, planes, _ = out_refs[0].shape
    tiles = moved_ref.shape[0]
    slab = planes // tiles
    size = slab * rows
    even = scalars[0]
    step = max(16, slab)
    for number, (blurred_ref, out_ref) in enumerate(zip(blurred_refs, out_refs)):
        edge = slice(number * half, (number + 1) * half)
        for at in range(0, planes, step):
            cells = [
                moved_ref[i, number * size : (number + 1) * size].reshape(slab, rows, LANES)
                for i in range(at // slab, (at + step) // slab)
            ]
            cells = cells[0] if len(cells) == 1 else jnp.concatenate(cells, axis=0)
            cells = jnp.swapaxes(cells, 0, 1) / blurred_ref[:, at : at + step]
            out_ref[:, at : at + step] = cells
            low, high = cells[:half], cells[rows - half :]
            inner_ref[edge, at : at + step] = jnp.where(even == 1, high, low)
            outer_ref[edge, at : at + step] = jnp.where(even == 1, low, high)
    if first:
        for number in range(packed.shape[0]):
            for source in range(tiles):
                at = count * size + number * slab
                packed[number, source * slab : (source + 1) * slab] = moved_ref[source, at : at + slab]
        per = LANES // SLOT
        values = []
        for r in range(rows):
            value = unpack(packed[r // per], r % per) / tail_ref[r]
            tail_out[r] = value
            if r < half or r >= rows - half:
                values.append(value)
        low, high = pack(values[:half]), pack(values[half:])
        inner_ref[count * half] = jnp.where(even == 1, high, low)
        outer_ref[count * half] = jnp.where(even == 1, low, high)


def ratio(scalars, moved, blurred, half, chunks, after):
    rows, planes, cells = blurred.shape
    first = 0 in chunks
    count = len(chunks)

    def column(block):
        return pl.BlockSpec((rows, planes, LANES), lambda i: (0, 0, block))

    edge = sds((half * count + (1 if first else 0), planes, LANES))
    whole = sds((rows, planes, LANES))
    outs = [whole] * count + [edge, edge] + ([whole] if first else [])
    columns = list(chunks) + ([cells // LANES - 1] if first else [])
    outs = pl.pallas_call(
        functools.partial(ratio_kernel, half, chunks, first),
        grid=(1,),
        in_specs=[SMEM, pl.BlockSpec(moved.shape, lambda i: (0, 0, 0))]
        + [column(block) for block in columns]
        + [ANY],
        out_specs=[pl.BlockSpec(out.shape, lambda i: (0, 0, 0)) for out in outs],
        out_shape=outs,
        scratch_shapes=[pltpu.VMEM((pl.cdiv(rows, LANES // SLOT), planes, LANES), F32)] if first else [],
        compiler_params=params(),
        cost_estimate=cost("ratio"),
        name="ratio",
    )(scalars, moved, *[blurred] * len(columns), after)
    return outs[:count], outs[count], outs[count + 1], outs[count + 2 :]


def back_kernel(taps, count, first, scalars, weights, inner, outer, along_z, along_x, *refs):
    owns, refs = refs[:count], refs[count:]
    tail, refs = (refs[0], refs[1:]) if first else (None, refs)
    before, refs = (None, refs) if first else (refs[:2], refs[2:])
    _, *refs = refs
    high_out, low_out, *quarters = refs[:6]
    buffers, halves, yz_high, yz_low, totals, sems, out_sems, spare, spare_sems = refs[6:]
    rows, planes, _ = owns[0].shape
    half = (taps - 1) // 2
    even = scalars[0]
    group = 4

    def blur_rows(buffer, planes_from, planes_count):
        def step_y(index, carry):
            planes_at = pl.multiple_of(planes_from + index * 16, 16)
            for r, (high, low) in blur_y(buffer, weights, taps, rows, planes_at, 0):
                lanes = slice((r % 2) * LANES, (r % 2 + 1) * LANES)
                halves[r // 2, pl.ds(planes_at, 16), lanes] = high
                halves[r // 2, pl.ds(planes + planes_at, 16), lanes] = low
            return carry

        lax.fori_loop(0, planes_count // 16, step_y, 0)

    def blur_planes(slot, number):
        def step_zx(index, carry):
            parts = []
            for g in range(group // 2):
                both = dot(along_z[...], halves[index * (group // 2) + g])
                both = both[:planes] + both[planes:]
                parts += [both[:, :LANES], both[:, LANES:]]
            mine = split(jnp.concatenate(parts, axis=0))
            at = pl.ds(index * group, group)
            for value, keep, last in zip(mine, (yz_high, yz_low), (high_out, low_out)):
                value = value.reshape(group, planes, LANES)
                if number == count - 1:
                    last[at] = value
                else:
                    keep[slot, at] = value
            if number >= 0:
                others = [before[0][at], before[1][at]] if slot is None else [yz_high[slot ^ 1, at], yz_low[slot ^ 1, at]]
                result = 0.0
                for own, other in zip(mine, others):
                    pair = jnp.concatenate([other.reshape(-1, LANES), own], axis=1)
                    result = result + dot(pair, along_x[number])
                result = result[:, :LANES] + result[:, LANES:]
                totals[pl.ds(number * rows + index * group, group)] = result.reshape(group, planes, LANES)
            return carry

        lax.fori_loop(0, rows // group, step_zx, 0)

    loads = [
        place_rows(even, own, inner, outer, number * half, buffers.at[number], sems.at[number], half)
        for number, own in enumerate(owns)
    ]
    if first:
        inner_at = jnp.where(even == 1, half + rows, 0)
        outer_at = jnp.where(even == 1, 0, half + rows)
        tail_loads = [
            pltpu.make_async_copy(tail, buffers.at[count, pl.ds(half, rows)], spare_sems.at[0]),
            pltpu.make_async_copy(inner.at[count * half], spare.at[0], spare_sems.at[1]),
            pltpu.make_async_copy(outer.at[count * half], spare.at[1], spare_sems.at[2]),
        ]
        start_all(tail_loads)
    for load in loads:
        for copies in load:
            start_all(copies)
    if first:
        wait_all(tail_loads)
        for number, at in enumerate((inner_at, outer_at)):
            for r in range(half):
                buffers[count, at + r] = unpack(spare[number], r)
        blur_rows(buffers.at[count], 0, planes)
        blur_planes(0, -1)
    size = planes // 4
    stores = []
    for number, load in enumerate(loads):
        step = planes // len(load)
        for block, copies in enumerate(load):
            wait_all(copies)
            blur_rows(buffers.at[number], block * step, step)
        blur_planes((number + 1) % 2 if first else None, number)
        for k, quarter in enumerate(quarters):
            start = pl.multiple_of((scalars[1] ^ k) * size, size)
            at = pl.ds(number * rows, rows)
            stores.append(
                pltpu.make_async_copy(totals.at[at, pl.ds(start, size)], quarter.at[at], out_sems.at[number, k])
            )
        start_all(stores[-4:])
    wait_all(stores)


def back(scalars, weights, owns, tail, inner, outer, along_z, along_x, before, chunks, after):
    rows, planes, _ = owns[0].shape
    taps = weights.shape[0]
    count = len(chunks)
    first = before is None
    square = pl.BlockSpec((count, 2 * LANES, 2 * LANES), lambda i: (chunks[0] // count, 0, 0))
    outs = pl.pallas_call(
        functools.partial(back_kernel, taps, count, first),
        grid=(1,),
        in_specs=[SMEM, SMEM, ANY, ANY, VMEM, square]
        + [ANY] * count
        + ([ANY] if first else [VMEM, VMEM])
        + [ANY],
        out_specs=[VMEM] * 2 + [ANY] * 4,
        out_shape=[sds((rows, planes, LANES), BF16)] * 2 + [sds((count * rows, planes // 4, LANES))] * 4,
        scratch_shapes=[
            pltpu.VMEM((count + (1 if first else 0), rows + taps - 1, planes, LANES), F32),
            pltpu.VMEM((rows // 2, 2 * planes, 2 * LANES), BF16),
            pltpu.VMEM((2, rows, planes, LANES), BF16),
            pltpu.VMEM((2, rows, planes, LANES), BF16),
            pltpu.VMEM((count * rows, planes, LANES), F32),
            pltpu.SemaphoreType.DMA((count, 3, 4)),
            pltpu.SemaphoreType.DMA((count, 4)),
            pltpu.VMEM((2, planes, LANES), F32),
            pltpu.SemaphoreType.DMA((3,)),
        ],
        compiler_params=params(),
        cost_estimate=cost("back"),
        name="back",
    )(
        scalars, weights, inner, outer, along_z, along_x, *owns, *(tail if first else before), after
    )
    return outs[:2], outs[2:]


def merge_kernel(count, scalars, estimate_ref, a, b, c, d, after, out_ref):
    step, rows, _ = estimate_ref.shape
    total = (a[...] + b[...]) + (c[...] + d[...])
    views = scalars[2].astype(F32)
    for number in range(count):
        lanes = slice(number * LANES, (number + 1) * LANES)
        mine = jnp.swapaxes(total[number * rows : (number + 1) * rows], 0, 1)
        out_ref[:, :, lanes] = estimate_ref[:, :, lanes] * mine / views


def merge(scalars, estimate, parts, chunks, after):
    _, size, _ = parts[0].shape
    rows = estimate.shape[1]
    count = len(chunks)
    step = 16
    steps = size // step
    piece = pl.BlockSpec((count * rows, step, LANES), lambda i, s: (0, i, 0))
    block = chunks[0] // count
    return pl.pallas_call(
        functools.partial(merge_kernel, count),
        grid_spec=pltpu.PrefetchScalarGridSpec(
            num_scalar_prefetch=1,
            grid=(steps,),
            in_specs=[
                pl.BlockSpec((step, rows, count * LANES), lambda i, s: (s[1] * steps + i, 0, block))
            ]
            + [piece] * 4
            + [ANY],
            out_specs=pl.BlockSpec((step, rows, count * LANES), lambda i, s: (i, 0, 0)),
        ),
        out_shape=sds((size, rows, count * LANES)),
        compiler_params=params(),
        cost_estimate=cost("merge"),
        name="merge",
    )(scalars, estimate, *parts, after)


def assemble_kernel(count, cells_at, scalars, *refs):
    pieces, out_ref, sems = refs[:count], refs[-2], refs[-1]
    size, _, width = pieces[0].shape
    copies = []
    for k, piece in enumerate(pieces):
        start = 0 if count == 1 else (scalars[1] ^ k) * size
        copies.append(
            pltpu.make_async_copy(
                piece, out_ref.at[pl.ds(start, size), :, pl.ds(cells_at, width)], sems.at[k]
            )
        )
    start_all(copies)
    wait_all(copies)


def assemble(scalars, pieces, shape, cells_at, result, after):
    earlier = [] if result is None else [result]
    count = len(pieces)
    return pl.pallas_call(
        functools.partial(assemble_kernel, count, cells_at),
        in_specs=[SMEM] + [VMEM] * count + [ANY] * (len(earlier) + 1),
        out_specs=ANY,
        out_shape=sds(shape),
        scratch_shapes=[pltpu.SemaphoreType.DMA((count,))],
        input_output_aliases={} if result is None else {count + 1: 0},
        compiler_params=params(),
        cost_estimate=cost("assemble"),
        name="assemble",
    )(scalars, *pieces, *earlier, after)


def taps_at(distance, profile):
    result = jnp.zeros(distance.shape, F32)
    for tap in range(profile.shape[1]):
        result = jnp.where(distance == tap, profile[0, tap], result)
    return result


def total_of(profile):
    total = profile[0, 0]
    for tap in range(1, profile.shape[1]):
        total = total + profile[0, tap]
    return total


def bands_kernel(scalars, profile_z, profile_y, profile_x, after, forward_z, back_z, high_x, low_x, back_x):
    planes = forward_z.shape[0] // 2
    cells = high_x.shape[0]
    half_z = (profile_z.shape[1] - 1) // 2
    lead = (profile_x.shape[1] - 1) // 2
    total_z, total_y, total_x = total_of(profile_z), total_of(profile_y), total_of(profile_x)
    row = lax.broadcasted_iota(jnp.int32, (planes, planes), 0)
    column = lax.broadcasted_iota(jnp.int32, (planes, planes), 1)
    for out, distance in ((forward_z, column - row), (back_z, row - column)):
        high, low = split(taps_at(distance + half_z, profile_z) / total_z / total_y)
        for side in (slice(0, planes), slice(planes, 2 * planes)):
            out[:planes, side] = high
            out[planes:, side] = low

    step = 32

    def step_x(index, carry):
        at = pl.multiple_of(index * step, step)
        row = lax.broadcasted_iota(jnp.int32, (step, cells), 0) + at
        column = lax.broadcasted_iota(jnp.int32, (step, cells), 1) + lead
        column = jnp.where(column >= cells, column - cells, column)
        high, low = split(taps_at(row - column + lead, profile_x) / total_x)
        high_x[pl.ds(at, step), :] = high
        low_x[pl.ds(at, step), :] = low
        return carry

    lax.fori_loop(0, cells // step, step_x, 0)
    row = lax.broadcasted_iota(jnp.int32, (2 * LANES, LANES), 0)
    column = lax.broadcasted_iota(jnp.int32, (2 * LANES, LANES), 1)
    matrix = taps_at(column + LANES - row, profile_x) / total_x * scalars[3].astype(F32)
    for block in range(back_x.shape[0]):
        source = row + ((block - 1) * LANES + lead)
        high, low = split(jnp.where((source >= 0) & (source < cells), matrix, 0.0))
        back_x[block, :, :LANES] = high
        back_x[block, :, LANES:] = low


def bands(scalars, profile_z, profile_y, profile_x, planes, cells, after):
    return pl.pallas_call(
        bands_kernel,
        in_specs=[SMEM] * 4 + [ANY],
        out_specs=[VMEM] * 5,
        out_shape=[
            sds((2 * planes, 2 * planes), BF16),
            sds((2 * planes, 2 * planes), BF16),
            sds((cells, cells), BF16),
            sds((cells, cells), BF16),
            sds((cells // LANES, 2 * LANES, 2 * LANES), BF16),
        ],
        compiler_params=params(),
        cost_estimate=cost("bands"),
        name="bands",
    )(scalars, profile_z, profile_y, profile_x, after)


def swap_views(cells, mask):
    return lax.ppermute(cells, "view", [(i, i ^ mask) for i in range(4)])


def on_device(estimate, view_stacks, profile_z, profile_y, profile_x, offsets, coverage):
    planes, rows, cells = estimate.shape
    half = (profile_y.shape[1] - 1) // 2
    lead = (profile_x.shape[1] - 1) // 2
    tiles = lax.axis_size("tile")
    tile = lax.axis_index("tile")
    view = lax.axis_index("view")
    chunks = cells // LANES
    even = (tile + 1) % 2
    groups = [tuple(range(chunks - 2))] + [(chunk,) for chunk in range(chunks - 2, chunks)]
    covered = lax.dynamic_index_in_dim(coverage[0], view, 0, keepdims=False)
    scalars = jnp.stack([even, view, jnp.sum(coverage[0]), covered]).astype(jnp.int32)
    inner_pairs = [(i, i ^ 1) for i in range(tiles)]
    outer_pairs = [(i, i + 1) for i in range(1, tiles - 1, 2)] + [(i + 1, i) for i in range(1, tiles - 1, 2)]

    def exchange(inner, outer):
        return lax.ppermute(inner, "tile", inner_pairs), lax.ppermute(outer, "tile", outer_pairs)

    def move(index, after):
        cells = registered[index] if after is None else gate([registered[index]], after)[0]
        return lax.all_to_all(cells, "tile", split_axis=0, concat_axis=0)

    def share(index, after):
        new = merge(scalars, estimate, parts[index], groups[index], after)
        if index < final:
            pieces[index] = [lax.all_gather(new, "view", axis=0, tiled=True)]
        else:
            pieces[index] = [new] + [swap_views(new, k) for k in (1, 2, 3)]
        return new

    def finish(index, after):
        return assemble(scalars, pieces[index], estimate.shape, groups[index][0] * LANES, result, after)

    final = len(groups) - 1
    places = jnp.stack([even, view]).astype(jnp.int32)
    rows_sent = edge_rows(places, estimate)
    inner, outer = exchange(*rows_sent)
    outers = [outer] + [swap_views(outer, k) for k in (1, 2, 3)]
    *registered, token = prep(offsets, view_stacks[0], tiles, lead, groups, rows_sent[0])
    moved = move(0, (outer,))
    transposed = swap(estimate, token)
    forward_z, back_z, high_x, low_x, back_x = bands(
        scalars, profile_z, profile_y, profile_x, planes, cells, transposed
    )
    inner, outer = swap_edges(places, inner, outers, half, back_z)
    blurred = forward(
        scalars, profile_y[0], transposed, inner, outer, forward_z, high_x, low_x, back_z
    )
    flipped = profile_y[0, ::-1]
    last, result, before = blurred, None, None
    parts, pieces = {}, {}
    for index, group in enumerate(groups):
        quotients, inner, outer, tail = ratio(scalars, moved, blurred, half, group, last)
        last = quotients[0]
        inner, outer = exchange(inner, outer)
        if index < final:
            moved = move(index + 1, (inner,))
        if index >= 1:
            last = share(index - 1, last)
        before, sums = back(
            scalars, flipped, quotients, tail, inner, outer, back_z, back_x, before, group, last
        )
        last = before[0]
        parts[index] = [sums[0]] + [swap_views(sums[k], k) for k in (1, 2, 3)]
        if index >= 2:
            result = finish(index - 2, last)
            last = result
    last = share(final, last)
    result = finish(final - 1, last)
    result = finish(final, last)
    return result


def solution(mesh):
    return jax.shard_map(
        on_device,
        mesh=mesh,
        in_specs=(
            P(None, "tile", None),
            P("view", "tile", None, None),
            P("view", None),
            P("view", None),
            P("view", None),
            P("view"),
            P("tile", None),
        ),
        out_specs=P(None, "tile", None),
        check_vma=False,
    )
```

```python
import functools

import jax
import jax.numpy as jnp
from jax import lax
from jax.experimental import pallas as pl
from jax.experimental.pallas import tpu as pltpu
from jax.sharding import PartitionSpec as P

LANES = 128
SLOT = 8
VMEM_MIB = 56
F32 = jnp.float32
BF16 = jnp.bfloat16
SMEM = pl.BlockSpec(memory_space=pltpu.SMEM)
VMEM = pl.BlockSpec(memory_space=pltpu.VMEM)
ANY = pl.BlockSpec(memory_space=pl.ANY)


MICROS = dict(prep=9, edge_rows=5, swap=8, swap_edges=6, gate=1, forward=30, ratio=5, back=60, bands=4, merge=30, assemble=10)


def cost(name):
    micros = MICROS[name]
    return pl.CostEstimate(flops=int(micros * 1.1e9), bytes_accessed=int(micros * 3.6e6), transcendentals=0)


def sds(shape, dtype=F32):
    return jax.ShapeDtypeStruct(shape, dtype)


def params():
    return pltpu.CompilerParams(vmem_limit_bytes=VMEM_MIB << 20)


def split(value):
    high = value.astype(BF16)
    return high, (value - high.astype(F32)).astype(BF16)


def dot(a, b):
    return jnp.dot(a, b, preferred_element_type=F32)


def pack(rows):
    lane = lax.broadcasted_iota(jnp.int32, rows[0].shape, 1)
    total = jnp.zeros(rows[0].shape, F32)
    for slot, row in enumerate(rows):
        moved = pltpu.roll(row, (SLOT * slot + SLOT) % LANES, 1)
        total = jnp.where((lane >= SLOT * slot) & (lane < SLOT * slot + SLOT), moved, total)
    return total


def unpack(packed, slot):
    lane = lax.broadcasted_iota(jnp.int32, packed.shape, 1)
    moved = pltpu.roll(packed, (2 * LANES - SLOT - SLOT * slot) % LANES, 1)
    return jnp.where(lane >= LANES - SLOT, moved, 0.0)


def prep_kernel(lead, groups, offsets, stack_ref, after, *out_refs):
    *out_refs, token_ref = out_refs
    token_ref[...] = jnp.zeros(token_ref.shape, F32)
    planes, rows, cells = stack_ref.shape
    offset = offsets[0]
    lane = lax.broadcasted_iota(jnp.int32, (1, 1, cells), 2)
    column = lane + lead
    column = jnp.where(column >= cells, column - cells, column)
    source = column + offset
    inside = (source >= 0) & (source < cells)
    shift = lax.rem(2 * cells - lead - offset, cells)
    rolled = pltpu.roll(stack_ref[...].reshape(planes * rows, cells), shift, 1)
    rolled = jnp.where(inside, rolled.reshape(planes, rows, cells), 0.0)
    size = planes * rows
    for group, out_ref in zip(groups, out_refs):
        for number, chunk in enumerate(group):
            values = rolled[:, :, chunk * LANES : (chunk + 1) * LANES]
            out_ref[0, number * size : (number + 1) * size] = values.reshape(size, LANES)
    tail = rolled[:, :, cells - LANES :]
    per = LANES // SLOT
    for number in range(pl.cdiv(rows, per)):
        at = len(groups[0]) * size + number * planes
        members = range(number * per, min((number + 1) * per, rows))
        out_refs[0][0, at : at + planes] = pack([tail[:, r, :] for r in members])


def prep(offsets, stack, tiles, lead, groups, after):
    planes, all_rows, cells = stack.shape
    rows = all_rows // tiles
    sizes = [len(group) * planes * rows for group in groups]
    sizes[0] += planes * pl.cdiv(rows, LANES // SLOT)
    return pl.pallas_call(
        functools.partial(prep_kernel, lead, groups),
        grid=(tiles,),
        in_specs=[SMEM, pl.BlockSpec((planes, rows, cells), lambda i: (0, i, 0)), ANY],
        out_specs=[pl.BlockSpec((1, size, LANES), lambda i: (i, 0, 0)) for size in sizes]
        + [pl.BlockSpec((8, LANES), lambda i: (0, 0))],
        out_shape=[sds((tiles, size, LANES)) for size in sizes] + [sds((8, LANES))],
        compiler_params=params(),
        cost_estimate=cost("prep"),
        name="prep",
    )(offsets, stack, after)


def copy_kernel(scalars, first_ref, second_ref, inner_ref, outer_ref):
    inner_ref[...] = first_ref[...]

    @pl.when(pl.program_id(0) == 0)
    def _():
        outer_ref[...] = second_ref[...]


def edge_rows(places, cells):
    planes, rows, width = cells.shape
    last = rows // 8 - 1
    step = planes // 4
    return pl.pallas_call(
        copy_kernel,
        grid_spec=pltpu.PrefetchScalarGridSpec(
            num_scalar_prefetch=1,
            grid=(planes // step,),
            in_specs=[
                pl.BlockSpec((step, 8, width), lambda i, s: (i, s[0] * last, 0)),
                pl.BlockSpec((step, 8, width), lambda i, s: (s[1], (1 - s[0]) * last, 0)),
            ],
            out_specs=[
                pl.BlockSpec((step, 8, width), lambda i, s: (i, 0, 0)),
                pl.BlockSpec((step, 8, width), lambda i, s: (0, 0, 0)),
            ],
        ),
        out_shape=[sds((planes, 8, width)), sds((step, 8, width))],
        compiler_params=params(),
        cost_estimate=cost("edge_rows"),
        name="edge_rows",
    )(places, cells, cells)


def swap_kernel(in_ref, after, out_ref):
    out_ref[...] = jnp.swapaxes(in_ref[...], 0, 1)


def swap(cells, after):
    planes, rows, width = cells.shape
    return pl.pallas_call(
        swap_kernel,
        grid=(planes // 16,),
        in_specs=[pl.BlockSpec((16, rows, width), lambda i: (i, 0, 0)), ANY],
        out_specs=pl.BlockSpec((rows, 16, width), lambda i: (0, i, 0)),
        out_shape=sds((rows, planes, width)),
        compiler_params=params(),
        cost_estimate=cost("swap"),
        name="swap",
    )(cells, after)


def swap_edges_kernel(half, scalars, inner_ref, a, b, c, d, after, inner_out, outer_out):
    even = scalars[0]
    inner = jnp.swapaxes(inner_ref[...], 0, 1)
    skip = inner.shape[0] - half
    inner_out[...] = jnp.where(even == 1, inner[:half], inner[skip:])
    for k, piece in enumerate((a, b, c, d)):

        @pl.when(pl.program_id(0) == k)
        def _():
            outer = jnp.swapaxes(piece[...], 0, 1)
            outer_out[...] = jnp.where(even == 1, outer[skip:], outer[:half])


def swap_edges(places, inner, pieces, half, after):
    planes, rows, width = inner.shape
    step = planes // 4
    return pl.pallas_call(
        functools.partial(swap_edges_kernel, half),
        grid_spec=pltpu.PrefetchScalarGridSpec(
            num_scalar_prefetch=1,
            grid=(4,),
            in_specs=[pl.BlockSpec((step, rows, width), lambda i, s: (s[1] ^ i, 0, 0))]
            + [pl.BlockSpec((step, rows, width), lambda i, s: (0, 0, 0))] * 4
            + [ANY],
            out_specs=[pl.BlockSpec((half, step, width), lambda i, s: (0, s[1] ^ i, 0))] * 2,
        ),
        out_shape=[sds((half, planes, width))] * 2,
        compiler_params=params(),
        cost_estimate=cost("swap_edges"),
        name="swap_edges",
    )(places, inner, *pieces, after)


def gate_kernel(*refs):
    pass


def gate(arrays, after):
    count = len(arrays)
    return pl.pallas_call(
        gate_kernel,
        in_specs=[ANY] * (count + len(after)),
        out_specs=[ANY] * count,
        out_shape=[sds(array.shape) for array in arrays],
        input_output_aliases={i: i for i in range(count)},
        compiler_params=params(),
        cost_estimate=cost("gate"),
        name="gate",
    )(*arrays, *after)


def place_rows(even, own, inner, outer, edges_at, buffer, sems, half):
    rows, planes, _ = own.shape
    blocks = sems.shape[1]
    step = planes // blocks
    inner_at = jnp.where(even == 1, half + rows, 0)
    outer_at = jnp.where(even == 1, 0, half + rows)
    copies = []
    for block in range(blocks):
        at = pl.ds(block * step, step)
        edge = pl.ds(edges_at, half)
        copies.append(
            [
                pltpu.make_async_copy(own.at[:, at], buffer.at[pl.ds(half, rows), at], sems.at[0, block]),
                pltpu.make_async_copy(inner.at[edge, at], buffer.at[pl.ds(inner_at, half), at], sems.at[1, block]),
                pltpu.make_async_copy(outer.at[edge, at], buffer.at[pl.ds(outer_at, half), at], sems.at[2, block]),
            ]
        )
    return copies


def start_all(copies):
    for copy in copies:
        copy.start()


def wait_all(copies):
    for copy in copies:
        copy.wait()


def blur_y(buffer, weights, taps, rows, planes_at, lanes_at):
    at = (pl.ds(planes_at, 16), pl.ds(lanes_at, LANES))
    cells = [buffer[(r, *at)] for r in range(rows + taps - 1)]
    for r in range(rows):
        total = weights[0] * cells[r]
        for tap in range(1, taps):
            total = total + weights[tap] * cells[r + tap]
        yield r, split(total)


def forward_kernel(taps, scalars, weights, own, inner, outer, along_z, high_x, low_x, after, out_ref, buffer, halves, sems):
    rows, planes, cells = own.shape
    half = (taps - 1) // 2
    blocks = place_rows(scalars[0], own, inner, outer, 0, buffer, sems, half)
    for copies in blocks:
        start_all(copies)
    step = planes // len(blocks)
    for block, copies in enumerate(blocks):
        wait_all(copies)

        def step_y(index, carry):
            planes_at = pl.multiple_of(block * step + (index // (cells // LANES)) * 16, 16)
            lanes_at = pl.multiple_of((index % (cells // LANES)) * LANES, LANES)
            for r, (high, low) in blur_y(buffer, weights, taps, rows, planes_at, lanes_at):
                halves[r, pl.ds(planes_at, 16), pl.ds(lanes_at, LANES)] = high
                halves[r, pl.ds(planes + planes_at, 16), pl.ds(lanes_at, LANES)] = low
            return carry

        lax.fori_loop(0, (step // 16) * (cells // LANES), step_y, 0)
    group = 4

    def step_zx(index, carry):
        parts = []
        for g in range(group):
            both = dot(along_z[...], halves[index * group + g])
            parts.append(both[:planes] + both[planes:])
        high, low = split(jnp.concatenate(parts, axis=0))
        result = dot(high, high_x[...]) + dot(low, high_x[...]) + dot(high, low_x[...])
        out_ref[pl.ds(index * group, group)] = result.reshape(group, planes, cells)
        return carry

    lax.fori_loop(0, rows // group, step_zx, 0, unroll=3)


def forward(even, weights, own, inner, outer, along_z, high_x, low_x, after):
    rows, planes, cells = own.shape
    taps = weights.shape[0]
    return pl.pallas_call(
        functools.partial(forward_kernel, taps),
        in_specs=[SMEM, SMEM, ANY, ANY, ANY, VMEM, VMEM, VMEM, ANY],
        out_specs=VMEM,
        out_shape=sds((rows, planes, cells)),
        scratch_shapes=[
            pltpu.VMEM((rows + taps - 1, planes, cells), F32),
            pltpu.VMEM((rows, 2 * planes, cells), BF16),
            pltpu.SemaphoreType.DMA((3, 4)),
        ],
        compiler_params=params(),
        cost_estimate=cost("forward"),
        name="forward",
    )(even, weights, own, inner, outer, along_z, high_x, low_x, after)


def edges_of(cells, half):
    return cells[:half], cells[cells.shape[0] - half :]


def ratio_kernel(half, chunks, first, scalars, moved_ref, *refs):
    count = len(chunks)
    blurred_refs, refs = refs[:count], refs[count:]
    if first:
        tail_ref, _, *refs = refs
        tail_out, packed = refs[count + 2 :]
    else:
        _, *refs = refs
    out_refs = refs[:count]
    inner_ref, outer_ref = refs[count : count + 2]
    rows, planes, _ = out_refs[0].shape
    tiles = moved_ref.shape[0]
    slab = planes // tiles
    size = slab * rows
    even = scalars[0]
    step = max(16, slab)
    for number, (blurred_ref, out_ref) in enumerate(zip(blurred_refs, out_refs)):
        edge = slice(number * half, (number + 1) * half)
        for at in range(0, planes, step):
            cells = [
                moved_ref[i, number * size : (number + 1) * size].reshape(slab, rows, LANES)
                for i in range(at // slab, (at + step) // slab)
            ]
            cells = cells[0] if len(cells) == 1 else jnp.concatenate(cells, axis=0)
            cells = jnp.swapaxes(cells, 0, 1) / blurred_ref[:, at : at + step]
            out_ref[:, at : at + step] = cells
            low, high = cells[:half], cells[rows - half :]
            inner_ref[edge, at : at + step] = jnp.where(even == 1, high, low)
            outer_ref[edge, at : at + step] = jnp.where(even == 1, low, high)
    if first:
        for number in range(packed.shape[0]):
            for source in range(tiles):
                at = count * size + number * slab
                packed[number, source * slab : (source + 1) * slab] = moved_ref[source, at : at + slab]
        per = LANES // SLOT
        values = []
        for r in range(rows):
            value = unpack(packed[r // per], r % per) / tail_ref[r]
            tail_out[r] = value
            if r < half or r >= rows - half:
                values.append(value)
        low, high = pack(values[:half]), pack(values[half:])
        inner_ref[count * half] = jnp.where(even == 1, high, low)
        outer_ref[count * half] = jnp.where(even == 1, low, high)


def ratio(scalars, moved, blurred, half, chunks, after):
    rows, planes, cells = blurred.shape
    first = 0 in chunks
    count = len(chunks)

    def column(block):
        return pl.BlockSpec((rows, planes, LANES), lambda i: (0, 0, block))

    edge = sds((half * count + (1 if first else 0), planes, LANES))
    whole = sds((rows, planes, LANES))
    outs = [whole] * count + [edge, edge] + ([whole] if first else [])
    columns = list(chunks) + ([cells // LANES - 1] if first else [])
    outs = pl.pallas_call(
        functools.partial(ratio_kernel, half, chunks, first),
        grid=(1,),
        in_specs=[SMEM, pl.BlockSpec(moved.shape, lambda i: (0, 0, 0))]
        + [column(block) for block in columns]
        + [ANY],
        out_specs=[pl.BlockSpec(out.shape, lambda i: (0, 0, 0)) for out in outs],
        out_shape=outs,
        scratch_shapes=[pltpu.VMEM((pl.cdiv(rows, LANES // SLOT), planes, LANES), F32)] if first else [],
        compiler_params=params(),
        cost_estimate=cost("ratio"),
        name="ratio",
    )(scalars, moved, *[blurred] * len(columns), after)
    return outs[:count], outs[count], outs[count + 1], outs[count + 2 :]


def back_kernel(taps, count, first, scalars, weights, inner, outer, along_z, along_x, *refs):
    owns, refs = refs[:count], refs[count:]
    tail, refs = (refs[0], refs[1:]) if first else (None, refs)
    before, refs = (None, refs) if first else (refs[:2], refs[2:])
    _, *refs = refs
    high_out, low_out, *quarters = refs[:6]
    buffers, halves, yz_high, yz_low, totals, sems, out_sems, spare, spare_sems = refs[6:]
    rows, planes, _ = owns[0].shape
    half = (taps - 1) // 2
    even = scalars[0]
    group = 4

    def blur_rows(buffer, planes_from, planes_count):
        def step_y(index, carry):
            planes_at = pl.multiple_of(planes_from + index * 16, 16)
            for r, (high, low) in blur_y(buffer, weights, taps, rows, planes_at, 0):
                lanes = slice((r % 2) * LANES, (r % 2 + 1) * LANES)
                halves[r // 2, pl.ds(planes_at, 16), lanes] = high
                halves[r // 2, pl.ds(planes + planes_at, 16), lanes] = low
            return carry

        lax.fori_loop(0, planes_count // 16, step_y, 0)

    def blur_planes(slot, number):
        def step_zx(index, carry):
            parts = []
            for g in range(group // 2):
                both = dot(along_z[...], halves[index * (group // 2) + g])
                both = both[:planes] + both[planes:]
                parts += [both[:, :LANES], both[:, LANES:]]
            mine = split(jnp.concatenate(parts, axis=0))
            at = pl.ds(index * group, group)
            for value, keep, last in zip(mine, (yz_high, yz_low), (high_out, low_out)):
                value = value.reshape(group, planes, LANES)
                if number == count - 1:
                    last[at] = value
                else:
                    keep[slot, at] = value
            if number >= 0:
                others = [before[0][at], before[1][at]] if slot is None else [yz_high[slot ^ 1, at], yz_low[slot ^ 1, at]]
                result = 0.0
                for own, other in zip(mine, others):
                    pair = jnp.concatenate([other.reshape(-1, LANES), own], axis=1)
                    result = result + dot(pair, along_x[number])
                result = result[:, :LANES] + result[:, LANES:]
                totals[pl.ds(number * rows + index * group, group)] = result.reshape(group, planes, LANES)
            return carry

        lax.fori_loop(0, rows // group, step_zx, 0, unroll=3)

    loads = [
        place_rows(even, own, inner, outer, number * half, buffers.at[number], sems.at[number], half)
        for number, own in enumerate(owns)
    ]
    if first:
        inner_at = jnp.where(even == 1, half + rows, 0)
        outer_at = jnp.where(even == 1, 0, half + rows)
        tail_loads = [
            pltpu.make_async_copy(tail, buffers.at[count, pl.ds(half, rows)], spare_sems.at[0]),
            pltpu.make_async_copy(inner.at[count * half], spare.at[0], spare_sems.at[1]),
            pltpu.make_async_copy(outer.at[count * half], spare.at[1], spare_sems.at[2]),
        ]
        start_all(tail_loads)
    for load in loads:
        for copies in load:
            start_all(copies)
    if first:
        wait_all(tail_loads)
        for number, at in enumerate((inner_at, outer_at)):
            for r in range(half):
                buffers[count, at + r] = unpack(spare[number], r)
        blur_rows(buffers.at[count], 0, planes)
        blur_planes(0, -1)
    size = planes // 4
    stores = []
    for number, load in enumerate(loads):
        step = planes // len(load)
        for block, copies in enumerate(load):
            wait_all(copies)
            blur_rows(buffers.at[number], block * step, step)
        blur_planes((number + 1) % 2 if first else None, number)
        for k, quarter in enumerate(quarters):
            start = pl.multiple_of((scalars[1] ^ k) * size, size)
            at = pl.ds(number * rows, rows)
            stores.append(
                pltpu.make_async_copy(totals.at[at, pl.ds(start, size)], quarter.at[at], out_sems.at[number, k])
            )
        start_all(stores[-4:])
    wait_all(stores)


def back(scalars, weights, owns, tail, inner, outer, along_z, along_x, before, chunks, after):
    rows, planes, _ = owns[0].shape
    taps = weights.shape[0]
    count = len(chunks)
    first = before is None
    square = pl.BlockSpec((count, 2 * LANES, 2 * LANES), lambda i: (chunks[0] // count, 0, 0))
    outs = pl.pallas_call(
        functools.partial(back_kernel, taps, count, first),
        grid=(1,),
        in_specs=[SMEM, SMEM, ANY, ANY, VMEM, square]
        + [ANY] * count
        + ([ANY] if first else [VMEM, VMEM])
        + [ANY],
        out_specs=[VMEM] * 2 + [ANY] * 4,
        out_shape=[sds((rows, planes, LANES), BF16)] * 2 + [sds((count * rows, planes // 4, LANES))] * 4,
        scratch_shapes=[
            pltpu.VMEM((count + (1 if first else 0), rows + taps - 1, planes, LANES), F32),
            pltpu.VMEM((rows // 2, 2 * planes, 2 * LANES), BF16),
            pltpu.VMEM((2, rows, planes, LANES), BF16),
            pltpu.VMEM((2, rows, planes, LANES), BF16),
            pltpu.VMEM((count * rows, planes, LANES), F32),
            pltpu.SemaphoreType.DMA((count, 3, 4)),
            pltpu.SemaphoreType.DMA((count, 4)),
            pltpu.VMEM((2, planes, LANES), F32),
            pltpu.SemaphoreType.DMA((3,)),
        ],
        compiler_params=params(),
        cost_estimate=cost("back"),
        name="back",
    )(
        scalars, weights, inner, outer, along_z, along_x, *owns, *(tail if first else before), after
    )
    return outs[:2], outs[2:]


def merge_kernel(count, scalars, estimate_ref, a, b, c, d, after, out_ref):
    step, rows, _ = estimate_ref.shape
    total = (a[...] + b[...]) + (c[...] + d[...])
    views = scalars[2].astype(F32)
    for number in range(count):
        lanes = slice(number * LANES, (number + 1) * LANES)
        mine = jnp.swapaxes(total[number * rows : (number + 1) * rows], 0, 1)
        out_ref[:, :, lanes] = estimate_ref[:, :, lanes] * mine / views


def merge(scalars, estimate, parts, chunks, after):
    _, size, _ = parts[0].shape
    rows = estimate.shape[1]
    count = len(chunks)
    step = 16
    steps = size // step
    piece = pl.BlockSpec((count * rows, step, LANES), lambda i, s: (0, i, 0))
    block = chunks[0] // count
    return pl.pallas_call(
        functools.partial(merge_kernel, count),
        grid_spec=pltpu.PrefetchScalarGridSpec(
            num_scalar_prefetch=1,
            grid=(steps,),
            in_specs=[
                pl.BlockSpec((step, rows, count * LANES), lambda i, s: (s[1] * steps + i, 0, block))
            ]
            + [piece] * 4
            + [ANY],
            out_specs=pl.BlockSpec((step, rows, count * LANES), lambda i, s: (i, 0, 0)),
        ),
        out_shape=sds((size, rows, count * LANES)),
        compiler_params=params(),
        cost_estimate=cost("merge"),
        name="merge",
    )(scalars, estimate, *parts, after)


def assemble_kernel(count, cells_at, scalars, *refs):
    pieces, out_ref, sems = refs[:count], refs[-2], refs[-1]
    size, _, width = pieces[0].shape
    copies = []
    for k, piece in enumerate(pieces):
        start = 0 if count == 1 else (scalars[1] ^ k) * size
        copies.append(
            pltpu.make_async_copy(
                piece, out_ref.at[pl.ds(start, size), :, pl.ds(cells_at, width)], sems.at[k]
            )
        )
    start_all(copies)
    wait_all(copies)


def assemble(scalars, pieces, shape, cells_at, result, after):
    earlier = [] if result is None else [result]
    count = len(pieces)
    return pl.pallas_call(
        functools.partial(assemble_kernel, count, cells_at),
        in_specs=[SMEM] + [VMEM] * count + [ANY] * (len(earlier) + 1),
        out_specs=ANY,
        out_shape=sds(shape),
        scratch_shapes=[pltpu.SemaphoreType.DMA((count,))],
        input_output_aliases={} if result is None else {count + 1: 0},
        compiler_params=params(),
        cost_estimate=cost("assemble"),
        name="assemble",
    )(scalars, *pieces, *earlier, after)


def taps_at(distance, profile):
    result = jnp.zeros(distance.shape, F32)
    for tap in range(profile.shape[1]):
        result = jnp.where(distance == tap, profile[0, tap], result)
    return result


def total_of(profile):
    total = profile[0, 0]
    for tap in range(1, profile.shape[1]):
        total = total + profile[0, tap]
    return total


def bands_kernel(scalars, profile_z, profile_y, profile_x, after, forward_z, back_z, high_x, low_x, back_x):
    planes = forward_z.shape[0] // 2
    cells = high_x.shape[0]
    half_z = (profile_z.shape[1] - 1) // 2
    lead = (profile_x.shape[1] - 1) // 2
    total_z, total_y, total_x = total_of(profile_z), total_of(profile_y), total_of(profile_x)
    row = lax.broadcasted_iota(jnp.int32, (planes, planes), 0)
    column = lax.broadcasted_iota(jnp.int32, (planes, planes), 1)
    for out, distance in ((forward_z, column - row), (back_z, row - column)):
        high, low = split(taps_at(distance + half_z, profile_z) / total_z / total_y)
        for side in (slice(0, planes), slice(planes, 2 * planes)):
            out[:planes, side] = high
            out[planes:, side] = low

    step = 32

    def step_x(index, carry):
        at = pl.multiple_of(index * step, step)
        row = lax.broadcasted_iota(jnp.int32, (step, cells), 0) + at
        column = lax.broadcasted_iota(jnp.int32, (step, cells), 1) + lead
        column = jnp.where(column >= cells, column - cells, column)
        high, low = split(taps_at(row - column + lead, profile_x) / total_x)
        high_x[pl.ds(at, step), :] = high
        low_x[pl.ds(at, step), :] = low
        return carry

    lax.fori_loop(0, cells // step, step_x, 0)
    row = lax.broadcasted_iota(jnp.int32, (2 * LANES, LANES), 0)
    column = lax.broadcasted_iota(jnp.int32, (2 * LANES, LANES), 1)
    matrix = taps_at(column + LANES - row, profile_x) / total_x * scalars[3].astype(F32)
    for block in range(back_x.shape[0]):
        source = row + ((block - 1) * LANES + lead)
        high, low = split(jnp.where((source >= 0) & (source < cells), matrix, 0.0))
        back_x[block, :, :LANES] = high
        back_x[block, :, LANES:] = low


def bands(scalars, profile_z, profile_y, profile_x, planes, cells, after):
    return pl.pallas_call(
        bands_kernel,
        in_specs=[SMEM] * 4 + [ANY],
        out_specs=[VMEM] * 5,
        out_shape=[
            sds((2 * planes, 2 * planes), BF16),
            sds((2 * planes, 2 * planes), BF16),
            sds((cells, cells), BF16),
            sds((cells, cells), BF16),
            sds((cells // LANES, 2 * LANES, 2 * LANES), BF16),
        ],
        compiler_params=params(),
        cost_estimate=cost("bands"),
        name="bands",
    )(scalars, profile_z, profile_y, profile_x, after)


def swap_views(cells, mask):
    return lax.ppermute(cells, "view", [(i, i ^ mask) for i in range(4)])


def on_device(estimate, view_stacks, profile_z, profile_y, profile_x, offsets, coverage):
    planes, rows, cells = estimate.shape
    half = (profile_y.shape[1] - 1) // 2
    lead = (profile_x.shape[1] - 1) // 2
    tiles = lax.axis_size("tile")
    tile = lax.axis_index("tile")
    view = lax.axis_index("view")
    chunks = cells // LANES
    even = (tile + 1) % 2
    groups = [tuple(range(chunks - 2))] + [(chunk,) for chunk in range(chunks - 2, chunks)]
    covered = lax.dynamic_index_in_dim(coverage[0], view, 0, keepdims=False)
    scalars = jnp.stack([even, view, jnp.sum(coverage[0]), covered]).astype(jnp.int32)
    inner_pairs = [(i, i ^ 1) for i in range(tiles)]
    outer_pairs = [(i, i + 1) for i in range(1, tiles - 1, 2)] + [(i + 1, i) for i in range(1, tiles - 1, 2)]

    def exchange(inner, outer):
        return lax.ppermute(inner, "tile", inner_pairs), lax.ppermute(outer, "tile", outer_pairs)

    def move(index, after):
        cells = registered[index] if after is None else gate([registered[index]], after)[0]
        return lax.all_to_all(cells, "tile", split_axis=0, concat_axis=0)

    def share(index, after):
        new = merge(scalars, estimate, parts[index], groups[index], after)
        if index < final:
            pieces[index] = [lax.all_gather(new, "view", axis=0, tiled=True)]
        else:
            pieces[index] = [new] + [swap_views(new, k) for k in (1, 2, 3)]
        return new

    def finish(index, after):
        return assemble(scalars, pieces[index], estimate.shape, groups[index][0] * LANES, result, after)

    final = len(groups) - 1
    places = jnp.stack([even, view]).astype(jnp.int32)
    rows_sent = edge_rows(places, estimate)
    inner, outer = exchange(*rows_sent)
    outers = [outer] + [swap_views(outer, k) for k in (1, 2, 3)]
    *registered, token = prep(offsets, view_stacks[0], tiles, lead, groups, rows_sent[0])
    moved = move(0, (outer,))
    transposed = swap(estimate, token)
    forward_z, back_z, high_x, low_x, back_x = bands(
        scalars, profile_z, profile_y, profile_x, planes, cells, transposed
    )
    inner, outer = swap_edges(places, inner, outers, half, back_z)
    blurred = forward(
        scalars, profile_y[0], transposed, inner, outer, forward_z, high_x, low_x, back_z
    )
    flipped = profile_y[0, ::-1]
    last, result, before = blurred, None, None
    parts, pieces = {}, {}
    for index, group in enumerate(groups):
        quotients, inner, outer, tail = ratio(scalars, moved, blurred, half, group, last)
        last = quotients[0]
        inner, outer = exchange(inner, outer)
        if index < final:
            moved = move(index + 1, (inner,))
        if index >= 1:
            last = share(index - 1, last)
        before, sums = back(
            scalars, flipped, quotients, tail, inner, outer, back_z, back_x, before, group, last
        )
        last = before[0]
        parts[index] = [sums[0]] + [swap_views(sums[k], k) for k in (1, 2, 3)]
        if index >= 2:
            result = finish(index - 2, last)
            last = result
    last = share(final, last)
    result = finish(final - 1, last)
    result = finish(final, last)
    return result


def solution(mesh):
    return jax.shard_map(
        on_device,
        mesh=mesh,
        in_specs=(
            P(None, "tile", None),
            P("view", "tile", None, None),
            P("view", None),
            P("view", None),
            P("view", None),
            P("view"),
            P("tile", None),
        ),
        out_specs=P(None, "tile", None),
        check_vma=False,
    )
```

```python
import functools

import jax
import jax.numpy as jnp
from jax import lax
from jax.experimental import pallas as pl
from jax.experimental.pallas import tpu as pltpu
from jax.sharding import PartitionSpec as P

LANES = 128
SLOT = 8
VMEM_MIB = 56
F32 = jnp.float32
BF16 = jnp.bfloat16
SMEM = pl.BlockSpec(memory_space=pltpu.SMEM)
VMEM = pl.BlockSpec(memory_space=pltpu.VMEM)
ANY = pl.BlockSpec(memory_space=pl.ANY)


MICROS = dict(prep=9, edge_rows=5, swap=8, swap_edges=6, gate=1, forward=30, ratio=5, back=60, bands=4, merge=30, assemble=10)


def cost(name):
    micros = MICROS[name]
    return pl.CostEstimate(flops=int(micros * 1.1e9), bytes_accessed=int(micros * 3.6e6), transcendentals=0)


def sds(shape, dtype=F32):
    return jax.ShapeDtypeStruct(shape, dtype)


def params():
    return pltpu.CompilerParams(vmem_limit_bytes=VMEM_MIB << 20)


def split(value):
    high = value.astype(BF16)
    return high, (value - high.astype(F32)).astype(BF16)


def dot(a, b):
    return jnp.dot(a, b, preferred_element_type=F32)


def pack(rows):
    lane = lax.broadcasted_iota(jnp.int32, rows[0].shape, 1)
    total = jnp.zeros(rows[0].shape, F32)
    for slot, row in enumerate(rows):
        moved = pltpu.roll(row, (SLOT * slot + SLOT) % LANES, 1)
        total = jnp.where((lane >= SLOT * slot) & (lane < SLOT * slot + SLOT), moved, total)
    return total


def unpack(packed, slot):
    lane = lax.broadcasted_iota(jnp.int32, packed.shape, 1)
    moved = pltpu.roll(packed, (2 * LANES - SLOT - SLOT * slot) % LANES, 1)
    return jnp.where(lane >= LANES - SLOT, moved, 0.0)


def prep_kernel(lead, groups, offsets, stack_ref, after, *out_refs):
    *out_refs, token_ref = out_refs
    token_ref[...] = jnp.zeros(token_ref.shape, F32)
    planes, rows, cells = stack_ref.shape
    offset = offsets[0]
    lane = lax.broadcasted_iota(jnp.int32, (1, 1, cells), 2)
    column = lane + lead
    column = jnp.where(column >= cells, column - cells, column)
    source = column + offset
    inside = (source >= 0) & (source < cells)
    shift = lax.rem(2 * cells - lead - offset, cells)
    rolled = pltpu.roll(stack_ref[...].reshape(planes * rows, cells), shift, 1)
    rolled = jnp.where(inside, rolled.reshape(planes, rows, cells), 0.0)
    size = planes * rows
    for group, out_ref in zip(groups, out_refs):
        for number, chunk in enumerate(group):
            values = rolled[:, :, chunk * LANES : (chunk + 1) * LANES]
            out_ref[0, number * size : (number + 1) * size] = values.reshape(size, LANES)
    tail = rolled[:, :, cells - LANES :]
    per = LANES // SLOT
    for number in range(pl.cdiv(rows, per)):
        at = len(groups[0]) * size + number * planes
        members = range(number * per, min((number + 1) * per, rows))
        out_refs[0][0, at : at + planes] = pack([tail[:, r, :] for r in members])


def prep(offsets, stack, tiles, lead, groups, after):
    planes, all_rows, cells = stack.shape
    rows = all_rows // tiles
    sizes = [len(group) * planes * rows for group in groups]
    sizes[0] += planes * pl.cdiv(rows, LANES // SLOT)
    return pl.pallas_call(
        functools.partial(prep_kernel, lead, groups),
        grid=(tiles,),
        in_specs=[SMEM, pl.BlockSpec((planes, rows, cells), lambda i: (0, i, 0)), ANY],
        out_specs=[pl.BlockSpec((1, size, LANES), lambda i: (i, 0, 0)) for size in sizes]
        + [pl.BlockSpec((8, LANES), lambda i: (0, 0))],
        out_shape=[sds((tiles, size, LANES)) for size in sizes] + [sds((8, LANES))],
        compiler_params=params(),
        cost_estimate=cost("prep"),
        name="prep",
    )(offsets, stack, after)


def copy_kernel(scalars, first_ref, second_ref, inner_ref, outer_ref):
    inner_ref[...] = first_ref[...]

    @pl.when(pl.program_id(0) == 0)
    def _():
        outer_ref[...] = second_ref[...]


def edge_rows(places, cells):
    planes, rows, width = cells.shape
    last = rows // 8 - 1
    step = planes // 4
    return pl.pallas_call(
        copy_kernel,
        grid_spec=pltpu.PrefetchScalarGridSpec(
            num_scalar_prefetch=1,
            grid=(planes // step,),
            in_specs=[
                pl.BlockSpec((step, 8, width), lambda i, s: (i, s[0] * last, 0)),
                pl.BlockSpec((step, 8, width), lambda i, s: (s[1], (1 - s[0]) * last, 0)),
            ],
            out_specs=[
                pl.BlockSpec((step, 8, width), lambda i, s: (i, 0, 0)),
                pl.BlockSpec((step, 8, width), lambda i, s: (0, 0, 0)),
            ],
        ),
        out_shape=[sds((planes, 8, width)), sds((step, 8, width))],
        compiler_params=params(),
        cost_estimate=cost("edge_rows"),
        name="edge_rows",
    )(places, cells, cells)


def swap_kernel(in_ref, after, out_ref):
    out_ref[...] = jnp.swapaxes(in_ref[...], 0, 1)


def swap(cells, after):
    planes, rows, width = cells.shape
    return pl.pallas_call(
        swap_kernel,
        grid=(planes // 16,),
        in_specs=[pl.BlockSpec((16, rows, width), lambda i: (i, 0, 0)), ANY],
        out_specs=pl.BlockSpec((rows, 16, width), lambda i: (0, i, 0)),
        out_shape=sds((rows, planes, width)),
        compiler_params=params(),
        cost_estimate=cost("swap"),
        name="swap",
    )(cells, after)


def swap_edges_kernel(half, scalars, inner_ref, a, b, c, d, after, inner_out, outer_out):
    even = scalars[0]
    inner = jnp.swapaxes(inner_ref[...], 0, 1)
    skip = inner.shape[0] - half
    inner_out[...] = jnp.where(even == 1, inner[:half], inner[skip:])
    for k, piece in enumerate((a, b, c, d)):

        @pl.when(pl.program_id(0) == k)
        def _():
            outer = jnp.swapaxes(piece[...], 0, 1)
            outer_out[...] = jnp.where(even == 1, outer[skip:], outer[:half])


def swap_edges(places, inner, pieces, half, after):
    planes, rows, width = inner.shape
    step = planes // 4
    return pl.pallas_call(
        functools.partial(swap_edges_kernel, half),
        grid_spec=pltpu.PrefetchScalarGridSpec(
            num_scalar_prefetch=1,
            grid=(4,),
            in_specs=[pl.BlockSpec((step, rows, width), lambda i, s: (s[1] ^ i, 0, 0))]
            + [pl.BlockSpec((step, rows, width), lambda i, s: (0, 0, 0))] * 4
            + [ANY],
            out_specs=[pl.BlockSpec((half, step, width), lambda i, s: (0, s[1] ^ i, 0))] * 2,
        ),
        out_shape=[sds((half, planes, width))] * 2,
        compiler_params=params(),
        cost_estimate=cost("swap_edges"),
        name="swap_edges",
    )(places, inner, *pieces, after)


def gate_kernel(*refs):
    pass


def gate(arrays, after):
    count = len(arrays)
    return pl.pallas_call(
        gate_kernel,
        in_specs=[ANY] * (count + len(after)),
        out_specs=[ANY] * count,
        out_shape=[sds(array.shape) for array in arrays],
        input_output_aliases={i: i for i in range(count)},
        compiler_params=params(),
        cost_estimate=cost("gate"),
        name="gate",
    )(*arrays, *after)


def place_rows(even, own, inner, outer, edges_at, buffer, sems, half):
    rows, planes, _ = own.shape
    blocks = sems.shape[1]
    step = planes // blocks
    inner_at = jnp.where(even == 1, half + rows, 0)
    outer_at = jnp.where(even == 1, 0, half + rows)
    copies = []
    for block in range(blocks):
        at = pl.ds(block * step, step)
        edge = pl.ds(edges_at, half)
        copies.append(
            [
                pltpu.make_async_copy(own.at[:, at], buffer.at[pl.ds(half, rows), at], sems.at[0, block]),
                pltpu.make_async_copy(inner.at[edge, at], buffer.at[pl.ds(inner_at, half), at], sems.at[1, block]),
                pltpu.make_async_copy(outer.at[edge, at], buffer.at[pl.ds(outer_at, half), at], sems.at[2, block]),
            ]
        )
    return copies


def start_all(copies):
    for copy in copies:
        copy.start()


def wait_all(copies):
    for copy in copies:
        copy.wait()


def blur_y(buffer, weights, taps, rows, planes_at, lanes_at):
    at = (pl.ds(planes_at, 16), pl.ds(lanes_at, LANES))
    cells = [buffer[(r, *at)] for r in range(rows + taps - 1)]
    for r in range(rows):
        total = weights[0] * cells[r]
        for tap in range(1, taps):
            total = total + weights[tap] * cells[r + tap]
        yield r, split(total)


def forward_kernel(taps, scalars, weights, own, inner, outer, along_z, high_x, low_x, after, out_ref, buffer, halves, sems):
    rows, planes, cells = own.shape
    half = (taps - 1) // 2
    blocks = place_rows(scalars[0], own, inner, outer, 0, buffer, sems, half)
    for copies in blocks:
        start_all(copies)
    step = planes // len(blocks)
    for block, copies in enumerate(blocks):
        wait_all(copies)

        def step_y(index, carry):
            planes_at = pl.multiple_of(block * step + (index // (cells // LANES)) * 16, 16)
            lanes_at = pl.multiple_of((index % (cells // LANES)) * LANES, LANES)
            for r, (high, low) in blur_y(buffer, weights, taps, rows, planes_at, lanes_at):
                halves[r, pl.ds(planes_at, 16), pl.ds(lanes_at, LANES)] = high
                halves[r, pl.ds(planes + planes_at, 16), pl.ds(lanes_at, LANES)] = low
            return carry

        lax.fori_loop(0, (step // 16) * (cells // LANES), step_y, 0)
    group = 4

    def step_zx(index, carry):
        parts = []
        for g in range(group):
            both = dot(along_z[...], halves[index * group + g])
            parts.append(both[:planes] + both[planes:])
        high, low = split(jnp.concatenate(parts, axis=0))
        result = dot(high, high_x[...]) + dot(low, high_x[...]) + dot(high, low_x[...])
        out_ref[pl.ds(index * group, group)] = result.reshape(group, planes, cells)
        return carry

    lax.fori_loop(0, rows // group, step_zx, 0, unroll=6)


def forward(even, weights, own, inner, outer, along_z, high_x, low_x, after):
    rows, planes, cells = own.shape
    taps = weights.shape[0]
    return pl.pallas_call(
        functools.partial(forward_kernel, taps),
        in_specs=[SMEM, SMEM, ANY, ANY, ANY, VMEM, VMEM, VMEM, ANY],
        out_specs=VMEM,
        out_shape=sds((rows, planes, cells)),
        scratch_shapes=[
            pltpu.VMEM((rows + taps - 1, planes, cells), F32),
            pltpu.VMEM((rows, 2 * planes, cells), BF16),
            pltpu.SemaphoreType.DMA((3, 4)),
        ],
        compiler_params=params(),
        cost_estimate=cost("forward"),
        name="forward",
    )(even, weights, own, inner, outer, along_z, high_x, low_x, after)


def edges_of(cells, half):
    return cells[:half], cells[cells.shape[0] - half :]


def ratio_kernel(half, chunks, first, scalars, moved_ref, *refs):
    count = len(chunks)
    blurred_refs, refs = refs[:count], refs[count:]
    if first:
        tail_ref, _, *refs = refs
        tail_out, packed = refs[count + 2 :]
    else:
        _, *refs = refs
    out_refs = refs[:count]
    inner_ref, outer_ref = refs[count : count + 2]
    rows, planes, _ = out_refs[0].shape
    tiles = moved_ref.shape[0]
    slab = planes // tiles
    size = slab * rows
    even = scalars[0]
    step = max(16, slab)
    for number, (blurred_ref, out_ref) in enumerate(zip(blurred_refs, out_refs)):
        edge = slice(number * half, (number + 1) * half)
        for at in range(0, planes, step):
            cells = [
                moved_ref[i, number * size : (number + 1) * size].reshape(slab, rows, LANES)
                for i in range(at // slab, (at + step) // slab)
            ]
            cells = cells[0] if len(cells) == 1 else jnp.concatenate(cells, axis=0)
            cells = jnp.swapaxes(cells, 0, 1) / blurred_ref[:, at : at + step]
            out_ref[:, at : at + step] = cells
            low, high = cells[:half], cells[rows - half :]
            inner_ref[edge, at : at + step] = jnp.where(even == 1, high, low)
            outer_ref[edge, at : at + step] = jnp.where(even == 1, low, high)
    if first:
        for number in range(packed.shape[0]):
            for source in range(tiles):
                at = count * size + number * slab
                packed[number, source * slab : (source + 1) * slab] = moved_ref[source, at : at + slab]
        per = LANES // SLOT
        values = []
        for r in range(rows):
            value = unpack(packed[r // per], r % per) / tail_ref[r]
            tail_out[r] = value
            if r < half or r >= rows - half:
                values.append(value)
        low, high = pack(values[:half]), pack(values[half:])
        inner_ref[count * half] = jnp.where(even == 1, high, low)
        outer_ref[count * half] = jnp.where(even == 1, low, high)


def ratio(scalars, moved, blurred, half, chunks, after):
    rows, planes, cells = blurred.shape
    first = 0 in chunks
    count = len(chunks)

    def column(block):
        return pl.BlockSpec((rows, planes, LANES), lambda i: (0, 0, block))

    edge = sds((half * count + (1 if first else 0), planes, LANES))
    whole = sds((rows, planes, LANES))
    outs = [whole] * count + [edge, edge] + ([whole] if first else [])
    columns = list(chunks) + ([cells // LANES - 1] if first else [])
    outs = pl.pallas_call(
        functools.partial(ratio_kernel, half, chunks, first),
        grid=(1,),
        in_specs=[SMEM, pl.BlockSpec(moved.shape, lambda i: (0, 0, 0))]
        + [column(block) for block in columns]
        + [ANY],
        out_specs=[pl.BlockSpec(out.shape, lambda i: (0, 0, 0)) for out in outs],
        out_shape=outs,
        scratch_shapes=[pltpu.VMEM((pl.cdiv(rows, LANES // SLOT), planes, LANES), F32)] if first else [],
        compiler_params=params(),
        cost_estimate=cost("ratio"),
        name="ratio",
    )(scalars, moved, *[blurred] * len(columns), after)
    return outs[:count], outs[count], outs[count + 1], outs[count + 2 :]


def back_kernel(taps, count, first, scalars, weights, inner, outer, along_z, along_x, *refs):
    owns, refs = refs[:count], refs[count:]
    tail, refs = (refs[0], refs[1:]) if first else (None, refs)
    before, refs = (None, refs) if first else (refs[:2], refs[2:])
    _, *refs = refs
    high_out, low_out, *quarters = refs[:6]
    buffers, halves, yz_high, yz_low, totals, sems, out_sems, spare, spare_sems = refs[6:]
    rows, planes, _ = owns[0].shape
    half = (taps - 1) // 2
    even = scalars[0]
    group = 4

    def blur_rows(buffer, planes_from, planes_count):
        def step_y(index, carry):
            planes_at = pl.multiple_of(planes_from + index * 16, 16)
            for r, (high, low) in blur_y(buffer, weights, taps, rows, planes_at, 0):
                lanes = slice((r % 2) * LANES, (r % 2 + 1) * LANES)
                halves[r // 2, pl.ds(planes_at, 16), lanes] = high
                halves[r // 2, pl.ds(planes + planes_at, 16), lanes] = low
            return carry

        lax.fori_loop(0, planes_count // 16, step_y, 0, unroll=2)

    def blur_planes(slot, number):
        def step_zx(index, carry):
            parts = []
            for g in range(group // 2):
                both = dot(along_z[...], halves[index * (group // 2) + g])
                both = both[:planes] + both[planes:]
                parts += [both[:, :LANES], both[:, LANES:]]
            mine = split(jnp.concatenate(parts, axis=0))
            at = pl.ds(index * group, group)
            for value, keep, last in zip(mine, (yz_high, yz_low), (high_out, low_out)):
                value = value.reshape(group, planes, LANES)
                if number == count - 1:
                    last[at] = value
                else:
                    keep[slot, at] = value
            if number >= 0:
                others = [before[0][at], before[1][at]] if slot is None else [yz_high[slot ^ 1, at], yz_low[slot ^ 1, at]]
                result = 0.0
                for own, other in zip(mine, others):
                    pair = jnp.concatenate([other.reshape(-1, LANES), own], axis=1)
                    result = result + dot(pair, along_x[number])
                result = result[:, :LANES] + result[:, LANES:]
                totals[pl.ds(number * rows + index * group, group)] = result.reshape(group, planes, LANES)
            return carry

        lax.fori_loop(0, rows // group, step_zx, 0, unroll=6)

    loads = [
        place_rows(even, own, inner, outer, number * half, buffers.at[number], sems.at[number], half)
        for number, own in enumerate(owns)
    ]
    if first:
        inner_at = jnp.where(even == 1, half + rows, 0)
        outer_at = jnp.where(even == 1, 0, half + rows)
        tail_loads = [
            pltpu.make_async_copy(tail, buffers.at[count, pl.ds(half, rows)], spare_sems.at[0]),
            pltpu.make_async_copy(inner.at[count * half], spare.at[0], spare_sems.at[1]),
            pltpu.make_async_copy(outer.at[count * half], spare.at[1], spare_sems.at[2]),
        ]
        start_all(tail_loads)
    for load in loads:
        for copies in load:
            start_all(copies)
    if first:
        wait_all(tail_loads)
        for number, at in enumerate((inner_at, outer_at)):
            for r in range(half):
                buffers[count, at + r] = unpack(spare[number], r)
        blur_rows(buffers.at[count], 0, planes)
        blur_planes(0, -1)
    size = planes // 4
    stores = []
    for number, load in enumerate(loads):
        step = planes // len(load)
        for block, copies in enumerate(load):
            wait_all(copies)
            blur_rows(buffers.at[number], block * step, step)
        blur_planes((number + 1) % 2 if first else None, number)
        for k, quarter in enumerate(quarters):
            start = pl.multiple_of((scalars[1] ^ k) * size, size)
            at = pl.ds(number * rows, rows)
            stores.append(
                pltpu.make_async_copy(totals.at[at, pl.ds(start, size)], quarter.at[at], out_sems.at[number, k])
            )
        start_all(stores[-4:])
    wait_all(stores)


def back(scalars, weights, owns, tail, inner, outer, along_z, along_x, before, chunks, after):
    rows, planes, _ = owns[0].shape
    taps = weights.shape[0]
    count = len(chunks)
    first = before is None
    square = pl.BlockSpec((count, 2 * LANES, 2 * LANES), lambda i: (chunks[0] // count, 0, 0))
    outs = pl.pallas_call(
        functools.partial(back_kernel, taps, count, first),
        grid=(1,),
        in_specs=[SMEM, SMEM, ANY, ANY, VMEM, square]
        + [ANY] * count
        + ([ANY] if first else [VMEM, VMEM])
        + [ANY],
        out_specs=[VMEM] * 2 + [ANY] * 4,
        out_shape=[sds((rows, planes, LANES), BF16)] * 2 + [sds((count * rows, planes // 4, LANES))] * 4,
        scratch_shapes=[
            pltpu.VMEM((count + (1 if first else 0), rows + taps - 1, planes, LANES), F32),
            pltpu.VMEM((rows // 2, 2 * planes, 2 * LANES), BF16),
            pltpu.VMEM((2, rows, planes, LANES), BF16),
            pltpu.VMEM((2, rows, planes, LANES), BF16),
            pltpu.VMEM((count * rows, planes, LANES), F32),
            pltpu.SemaphoreType.DMA((count, 3, 4)),
            pltpu.SemaphoreType.DMA((count, 4)),
            pltpu.VMEM((2, planes, LANES), F32),
            pltpu.SemaphoreType.DMA((3,)),
        ],
        compiler_params=params(),
        cost_estimate=cost("back"),
        name="back",
    )(
        scalars, weights, inner, outer, along_z, along_x, *owns, *(tail if first else before), after
    )
    return outs[:2], outs[2:]


def merge_kernel(count, scalars, estimate_ref, a, b, c, d, after, out_ref):
    step, rows, _ = estimate_ref.shape
    total = (a[...] + b[...]) + (c[...] + d[...])
    views = scalars[2].astype(F32)
    for number in range(count):
        lanes = slice(number * LANES, (number + 1) * LANES)
        mine = jnp.swapaxes(total[number * rows : (number + 1) * rows], 0, 1)
        out_ref[:, :, lanes] = estimate_ref[:, :, lanes] * mine / views


def merge(scalars, estimate, parts, chunks, after):
    _, size, _ = parts[0].shape
    rows = estimate.shape[1]
    count = len(chunks)
    step = 16
    steps = size // step
    piece = pl.BlockSpec((count * rows, step, LANES), lambda i, s: (0, i, 0))
    block = chunks[0] // count
    return pl.pallas_call(
        functools.partial(merge_kernel, count),
        grid_spec=pltpu.PrefetchScalarGridSpec(
            num_scalar_prefetch=1,
            grid=(steps,),
            in_specs=[
                pl.BlockSpec((step, rows, count * LANES), lambda i, s: (s[1] * steps + i, 0, block))
            ]
            + [piece] * 4
            + [ANY],
            out_specs=pl.BlockSpec((step, rows, count * LANES), lambda i, s: (i, 0, 0)),
        ),
        out_shape=sds((size, rows, count * LANES)),
        compiler_params=params(),
        cost_estimate=cost("merge"),
        name="merge",
    )(scalars, estimate, *parts, after)


def assemble_kernel(count, cells_at, scalars, *refs):
    pieces, out_ref, sems = refs[:count], refs[-2], refs[-1]
    size, _, width = pieces[0].shape
    copies = []
    for k, piece in enumerate(pieces):
        start = 0 if count == 1 else (scalars[1] ^ k) * size
        copies.append(
            pltpu.make_async_copy(
                piece, out_ref.at[pl.ds(start, size), :, pl.ds(cells_at, width)], sems.at[k]
            )
        )
    start_all(copies)
    wait_all(copies)


def assemble(scalars, pieces, shape, cells_at, result, after):
    earlier = [] if result is None else [result]
    count = len(pieces)
    return pl.pallas_call(
        functools.partial(assemble_kernel, count, cells_at),
        in_specs=[SMEM] + [VMEM] * count + [ANY] * (len(earlier) + 1),
        out_specs=ANY,
        out_shape=sds(shape),
        scratch_shapes=[pltpu.SemaphoreType.DMA((count,))],
        input_output_aliases={} if result is None else {count + 1: 0},
        compiler_params=params(),
        cost_estimate=cost("assemble"),
        name="assemble",
    )(scalars, *pieces, *earlier, after)


def taps_at(distance, profile):
    result = jnp.zeros(distance.shape, F32)
    for tap in range(profile.shape[1]):
        result = jnp.where(distance == tap, profile[0, tap], result)
    return result


def total_of(profile):
    total = profile[0, 0]
    for tap in range(1, profile.shape[1]):
        total = total + profile[0, tap]
    return total


def bands_kernel(scalars, profile_z, profile_y, profile_x, after, forward_z, back_z, high_x, low_x, back_x):
    planes = forward_z.shape[0] // 2
    cells = high_x.shape[0]
    half_z = (profile_z.shape[1] - 1) // 2
    lead = (profile_x.shape[1] - 1) // 2
    total_z, total_y, total_x = total_of(profile_z), total_of(profile_y), total_of(profile_x)
    row = lax.broadcasted_iota(jnp.int32, (planes, planes), 0)
    column = lax.broadcasted_iota(jnp.int32, (planes, planes), 1)
    for out, distance in ((forward_z, column - row), (back_z, row - column)):
        high, low = split(taps_at(distance + half_z, profile_z) / total_z / total_y)
        for side in (slice(0, planes), slice(planes, 2 * planes)):
            out[:planes, side] = high
            out[planes:, side] = low

    step = 32

    def step_x(index, carry):
        at = pl.multiple_of(index * step, step)
        row = lax.broadcasted_iota(jnp.int32, (step, cells), 0) + at
        column = lax.broadcasted_iota(jnp.int32, (step, cells), 1) + lead
        column = jnp.where(column >= cells, column - cells, column)
        high, low = split(taps_at(row - column + lead, profile_x) / total_x)
        high_x[pl.ds(at, step), :] = high
        low_x[pl.ds(at, step), :] = low
        return carry

    lax.fori_loop(0, cells // step, step_x, 0)
    row = lax.broadcasted_iota(jnp.int32, (2 * LANES, LANES), 0)
    column = lax.broadcasted_iota(jnp.int32, (2 * LANES, LANES), 1)
    matrix = taps_at(column + LANES - row, profile_x) / total_x * scalars[3].astype(F32)
    for block in range(back_x.shape[0]):
        source = row + ((block - 1) * LANES + lead)
        high, low = split(jnp.where((source >= 0) & (source < cells), matrix, 0.0))
        back_x[block, :, :LANES] = high
        back_x[block, :, LANES:] = low


def bands(scalars, profile_z, profile_y, profile_x, planes, cells, after):
    return pl.pallas_call(
        bands_kernel,
        in_specs=[SMEM] * 4 + [ANY],
        out_specs=[VMEM] * 5,
        out_shape=[
            sds((2 * planes, 2 * planes), BF16),
            sds((2 * planes, 2 * planes), BF16),
            sds((cells, cells), BF16),
            sds((cells, cells), BF16),
            sds((cells // LANES, 2 * LANES, 2 * LANES), BF16),
        ],
        compiler_params=params(),
        cost_estimate=cost("bands"),
        name="bands",
    )(scalars, profile_z, profile_y, profile_x, after)


def swap_views(cells, mask):
    return lax.ppermute(cells, "view", [(i, i ^ mask) for i in range(4)])


def on_device(estimate, view_stacks, profile_z, profile_y, profile_x, offsets, coverage):
    planes, rows, cells = estimate.shape
    half = (profile_y.shape[1] - 1) // 2
    lead = (profile_x.shape[1] - 1) // 2
    tiles = lax.axis_size("tile")
    tile = lax.axis_index("tile")
    view = lax.axis_index("view")
    chunks = cells // LANES
    even = (tile + 1) % 2
    groups = [tuple(range(chunks - 2))] + [(chunk,) for chunk in range(chunks - 2, chunks)]
    covered = lax.dynamic_index_in_dim(coverage[0], view, 0, keepdims=False)
    scalars = jnp.stack([even, view, jnp.sum(coverage[0]), covered]).astype(jnp.int32)
    inner_pairs = [(i, i ^ 1) for i in range(tiles)]
    outer_pairs = [(i, i + 1) for i in range(1, tiles - 1, 2)] + [(i + 1, i) for i in range(1, tiles - 1, 2)]

    def exchange(inner, outer):
        return lax.ppermute(inner, "tile", inner_pairs), lax.ppermute(outer, "tile", outer_pairs)

    def move(index, after):
        cells = registered[index] if after is None else gate([registered[index]], after)[0]
        return lax.all_to_all(cells, "tile", split_axis=0, concat_axis=0)

    def share(index, after):
        new = merge(scalars, estimate, parts[index], groups[index], after)
        if index < final:
            pieces[index] = [lax.all_gather(new, "view", axis=0, tiled=True)]
        else:
            pieces[index] = [new] + [swap_views(new, k) for k in (1, 2, 3)]
        return new

    def finish(index, after):
        return assemble(scalars, pieces[index], estimate.shape, groups[index][0] * LANES, result, after)

    final = len(groups) - 1
    places = jnp.stack([even, view]).astype(jnp.int32)
    rows_sent = edge_rows(places, estimate)
    inner, outer = exchange(*rows_sent)
    outers = [outer] + [swap_views(outer, k) for k in (1, 2, 3)]
    *registered, token = prep(offsets, view_stacks[0], tiles, lead, groups, rows_sent[0])
    moved = move(0, (outer,))
    transposed = swap(estimate, token)
    forward_z, back_z, high_x, low_x, back_x = bands(
        scalars, profile_z, profile_y, profile_x, planes, cells, transposed
    )
    inner, outer = swap_edges(places, inner, outers, half, back_z)
    blurred = forward(
        scalars, profile_y[0], transposed, inner, outer, forward_z, high_x, low_x, back_z
    )
    flipped = profile_y[0, ::-1]
    last, result, before = blurred, None, None
    parts, pieces = {}, {}
    for index, group in enumerate(groups):
        quotients, inner, outer, tail = ratio(scalars, moved, blurred, half, group, last)
        last = quotients[0]
        inner, outer = exchange(inner, outer)
        if index < final:
            moved = move(index + 1, (inner,))
        if index >= 1:
            last = share(index - 1, last)
        before, sums = back(
            scalars, flipped, quotients, tail, inner, outer, back_z, back_x, before, group, last
        )
        last = before[0]
        parts[index] = [sums[0]] + [swap_views(sums[k], k) for k in (1, 2, 3)]
        if index >= 2:
            result = finish(index - 2, last)
            last = result
    last = share(final, last)
    result = finish(final - 1, last)
    result = finish(final, last)
    return result


def solution(mesh):
    return jax.shard_map(
        on_device,
        mesh=mesh,
        in_specs=(
            P(None, "tile", None),
            P("view", "tile", None, None),
            P("view", None),
            P("view", None),
            P("view", None),
            P("view"),
            P("tile", None),
        ),
        out_specs=P(None, "tile", None),
        check_vma=False,
    )
```
